512 devices in a mesh: rep: 16 (over x, y), fsdp: 32 (over z, core).
Axes of the slice: x: 4, y: 4, z: 16, core: 2. Of those that a mesh axis runs over, the one named last changes fastest.
Arguments:
- grads: bfloat16 [16, 4096, 5120], P('rep', 'fsdp'), may hold values from -6 to 6
- errors: bfloat16 [16, 4096, 5120], P('rep', 'fsdp'), may hold values from -4 to 4
- q_start: float32 [64, 5120], replicated, may hold values from -6 to 6
Outputs:
- new_errors: bfloat16 [16, 4096, 5120], P('rep', 'fsdp')
- factor_q: float32 [64, 5120], replicated
The draws below stay inside these ranges and needn't reach their ends.
All inputs are finite; a program needn't handle non-finite values.
Results may differ from the reference program's by a relative error of at most 0.001.
Values sent between devices are 32-bit elements; how exact they have to be, the bound alone decides.
No kernel may reach another device: no remote copies, remote signals or barrier semaphores. Data moves between devices by JAX's collectives and lax.ppermute only.
A program may use at most 64 MiB of HBM per device.

```python
import jax
import jax.numpy as jnp
from jax import lax

D = 4096
FF = 5120
R = 64
ITERS = 3
REPS = 16


def block_scale(key, dims, pieces, low, top_value):
    def one(dim, blocks):
        heights = jax.random.uniform(jax.random.fold_in(jax.random.fold_in(key, 6), dim), (blocks,), jnp.float32, low / len(pieces), top_value / len(pieces))
        return jnp.repeat(jnp.exp(heights), dims[dim] // blocks).reshape((-1,) + (1,) * (len(dims) - dim - 1))

    factor_of = one(*pieces[0])
    for cut in pieces[1:]:
        factor_of = factor_of * one(*cut)
    return factor_of


def centred(key, dims, spread, most, pieces=(), kind=jnp.bfloat16):
    result = jax.random.normal(key, dims, jnp.float32) * spread
    if len(pieces) > 0:
        result = block_scale(key, dims, pieces, -0.22, 0.18) * result
    return jnp.clip(result, min=-most, max=most).astype(kind)


def setup_inputs(seed: int = 0) -> dict:
    keys = jax.random.split(jax.random.key(seed), 4)
    grads = centred(keys[0], (REPS, D, FF), 1.0, 6.0, ((0, 16), (1, 32)))
    errors = centred(keys[1], (REPS, D, FF), 0.5, 4.0, ((0, 16), (1, 32)))
    q_start = centred(keys[2], (R, FF), 1.0, 6.0, (), jnp.float32)
    return {"grads": grads, "errors": errors, "q_start": q_start}


def orthonormal(left):
    for turn in range(2):
        gram = jnp.dot(left.T.astype(jnp.float32), left.astype(jnp.float32), precision=lax.Precision.HIGHEST, preferred_element_type=jnp.float32)
        lower = jnp.linalg.cholesky(gram)
        left = lax.linalg.triangular_solve(lower, left, left_side=False, lower=True, transpose_a=True)
    return left

def reference(grads, errors, q_start):

    def merged_of(index):
        return grads[index].astype(jnp.float32) + errors[index].astype(jnp.float32)
    indices = jnp.arange(REPS, dtype=jnp.int32)
    factor_q = q_start
    basis = jnp.zeros((D, R), jnp.float32)
    for step in range(ITERS):

        def add_left(total, index):
            merged = merged_of(index)
            term = lax.dot_general(merged.astype(jnp.float32), factor_q.astype(jnp.float32), (((1,), (1,)), ((), ())), precision=lax.Precision.HIGHEST, preferred_element_type=jnp.float32)
            return (total + term, None)
        left, unused = lax.scan(add_left, jnp.zeros((D, R), jnp.float32), indices)
        basis = orthonormal(left)

        def add_right(total, index):
            merged = merged_of(index)
            term = lax.dot_general(basis.astype(jnp.float32), merged.astype(jnp.float32), (((0,), (0,)), ((), ())), precision=lax.Precision.HIGHEST, preferred_element_type=jnp.float32)
            return (total + term, None)
        right, unused = lax.scan(add_right, jnp.zeros((R, FF), jnp.float32), indices)
        factor_q = right * (1.0 / REPS)

    def residual_of(index):
        product = jnp.dot(basis.astype(jnp.float32), factor_q.astype(jnp.float32), precision=lax.Precision.HIGHEST, preferred_element_type=jnp.float32)
        return (merged_of(index) - product).astype(jnp.bfloat16)
    new_errors = lax.map(residual_of, indices)
    return (new_errors, factor_q)
```

```python
import jax
import jax.numpy as jnp
from jax import lax
from jax.experimental import pallas as pl
from jax.experimental.pallas import tpu as pltpu
from jax.sharding import Mesh, PartitionSpec as P

ITERS = 3
F32 = jnp.float32
BF16 = jnp.bfloat16
LANES = 128
VMEM = 56 * 1024 * 1024
NT = (((1,), (1,)), ((), ()))
NN = (((1,), (0,)), ((), ()))


def dot(a, b, dims):
    return lax.dot_general(a, b, dims, preferred_element_type=F32)


def split2(x):
    high = x.astype(BF16)
    return high, (x - high.astype(F32)).astype(BF16)


def split3(x):
    high = x.astype(BF16)
    rest = x - high.astype(F32)
    mid = rest.astype(BF16)
    return high, mid, (rest - mid.astype(F32)).astype(BF16)


def params():
    return pltpu.CompilerParams(vmem_limit_bytes=VMEM)


def start_kernel(grads, errors, q_start, out):
    reps, tall, rows = out.shape
    rank, width = q_start.shape
    cut = width // reps
    extra = rank // reps
    left = jnp.zeros((2 * rank, rows), F32)
    for i in range(reps // 2):
        span = pl.ds(2 * cut * i, 2 * cut)
        g, e = grads[:, span], errors[:, span]
        turned = (g.astype(F32) + e.astype(F32)).T
        out[2 * i, :cut, :] = turned[:cut]
        out[2 * i + 1, :cut, :] = turned[cut:]
        high, low = split2(q_start[:, span])
        both = jnp.concatenate([high, low], axis=0)
        left = left + (dot(both, g, NT) + dot(both, e, NT))
    left = left[:rank] + left[rank:]
    for i in range(reps):
        out[i, cut : cut + extra, :] = left[extra * i : extra * (i + 1)]
        out[i, cut + extra :, :] = jnp.zeros((tall - cut - extra, rows), F32)


def start(grads, errors, q_start, reps):
    rows, width = grads.shape
    tall = width // reps + 8
    return pl.pallas_call(
        start_kernel,
        out_shape=jax.ShapeDtypeStruct((reps, tall, rows), F32),
        compiler_params=params(),
        name="start",
    )(grads, errors, q_start)


def parts_kernel(flag, own, other, high, low):
    first = flag[0] == 0
    for core in range(2):
        x = jnp.where(first, own[0], other[0]) if core == 0 else jnp.where(first, other[0], own[0])
        high[core], low[core] = split2(x)


def parts(flag, own, other):
    length, cut, rows = own.shape
    piece = pl.BlockSpec((1, cut, rows), lambda j: (j, 0, 0))
    result = pl.BlockSpec((2, cut, rows), lambda j: (0, 0, j))
    shape = jax.ShapeDtypeStruct((2, cut, length * rows), BF16)
    return pl.pallas_call(
        parts_kernel,
        grid=(length,),
        in_specs=[pl.BlockSpec(memory_space=pltpu.SMEM), piece, piece],
        out_specs=[result, result],
        out_shape=[shape, shape],
        compiler_params=params(),
        name="parts",
    )(flag, own, other)


def inverse_factor(gram_twice):
    rank, wide = gram_twice.shape
    step = 8
    count = rank // step
    row = lax.broadcasted_iota(jnp.int32, (step, wide), 0)
    col = lax.broadcasted_iota(jnp.int32, (step, wide), 1)
    a = []
    for b in range(count):
        unit = (col == row + (rank + b * step)).astype(F32)
        a.append(jnp.where(col < rank, gram_twice[b * step : (b + 1) * step], unit))
    for k in range(rank):
        block, inside = divmod(k, step)
        line = a[block][inside : inside + 1, :]
        line = line * (1.0 / line[:, k : k + 1])
        for b in range(block, count):
            factor = a[b][:, k : k + 1]
            if b == block:
                factor = jnp.where(row[:, :1] > inside, factor, 0.0)
            a[b] = a[b] - factor * line
    done = []
    for b in range(count):
        diagonal = jnp.sum(jnp.where(col == row + b * step, a[b], 0.0), axis=1, keepdims=True)
        done.append(jnp.where(col < rank, 0.0, a[b] * lax.rsqrt(diagonal)))
    w = jnp.concatenate(done, axis=0)
    return w + pltpu.roll(w, rank, 1)


def gram_of(held, chunk):
    rank = held.shape[0] // 4
    total = jnp.zeros((3 * rank, 4 * rank), F32)
    for at in range(0, held.shape[1], chunk):
        x = held[:, at : at + chunk]
        total = total + dot(x[: 3 * rank], x, NT)
    total = total[:rank] + (total[rank : 2 * rank] + total[2 * rank :])
    near, far = total[:, : 2 * rank], total[:, 2 * rank :]
    return near + pltpu.roll(near, rank, 1) + far


def put(held, at, x):
    rank, n = x.shape
    high, mid, low = split3(x)
    span = slice(at, at + n)
    held[:rank, span] = high
    held[rank : 2 * rank, span] = mid
    held[2 * rank : 3 * rank, span] = low
    held[3 * rank :, span] = low


def weights(w):
    rank = w.shape[0]
    col = lax.broadcasted_iota(jnp.int32, w.shape, 1)
    once = jnp.where(col < rank, w, 0.0)
    wide = jnp.concatenate([w, once], axis=1)
    return jnp.concatenate(split3(wide), axis=0)


def right_of(held, high, low, chunk):
    rank = held.shape[0] // 4
    cut, half = high.shape[1:]
    one = jnp.zeros((2 * rank, cut), F32)
    two = jnp.zeros((rank, cut), F32)
    for core in range(2):
        for at in range(0, half, chunk):
            x = held[: 2 * rank, core * half + at : core * half + at + chunk]
            one = one + dot(x, high[core, :, at : at + chunk], NT)
            two = two + dot(x[:rank], low[core, :, at : at + chunk], NT)
    return one[:rank] + (one[rank:] + two)


def orth_and_right(flag, own, other, high, low, held):
    length, rank, rows = own.shape
    chunk = 512
    first = flag[0] == 0
    for core in range(2):
        for j in range(length):
            x = jnp.where(first, own[j], other[j]) if core == 0 else jnp.where(first, other[j], own[j])
            put(held, (core * length + j) * rows, x)
    left = weights(inverse_factor(gram_of(held, chunk)))
    for at in range(0, held.shape[1], chunk):
        y = dot(left, held[:, at : at + chunk], NN)
        put(held, at, y[:rank] + (y[rank : 2 * rank] + y[2 * rank :]))
    second = inverse_factor(gram_of(held, chunk))
    right = right_of(held, high, low, chunk)
    right = jnp.dot(second[:, :rank], right, precision=lax.Precision.HIGHEST, preferred_element_type=F32)
    return second, right


def step_kernel(scale, flag, mine, own, other, high, low, out, held):
    length, rank, rows = own.shape
    _, right = orth_and_right(flag, own, other, high, low, held)
    q_high, q_low = split2(right * scale)
    both = jnp.concatenate([q_high, q_low], axis=0)
    core = mine[0]
    for j in range(length):
        span = slice(j * rows, (j + 1) * rows)
        one = dot(both, high[core, :, span], NN)
        out[j] = one[:rank] + (one[rank:] + dot(q_high, low[core, :, span], NN))


def last_kernel(scale, flag, place, own, other, high, low, out, basis, held):
    length, rank, rows = own.shape
    second, right = orth_and_right(flag, own, other, high, low, held)
    out[:, : right.shape[1]] = right * scale
    out[:, right.shape[1] :] = jnp.zeros((rank, out.shape[1] - right.shape[1]), F32)
    at = pl.multiple_of(place[0] * rows, rows)
    y = dot(weights(second), held[:, pl.ds(at, rows)], NN)
    basis[...] = y[:rank] + (y[rank : 2 * rank] + y[2 * rank :])


def iterate(scale, flag, index, own, other, high, low, last):
    length, rank, rows = own.shape
    cut = high.shape[1]
    if last:
        wide = -(-cut // LANES) * LANES
        out_shape = [jax.ShapeDtypeStruct((rank, wide), F32), jax.ShapeDtypeStruct((rank, rows), F32)]
    else:
        out_shape = jax.ShapeDtypeStruct((length, rank, rows), F32)
    kernel = last_kernel if last else step_kernel
    smem = pl.BlockSpec(memory_space=pltpu.SMEM)
    vmem = pl.BlockSpec(memory_space=pltpu.VMEM)
    return pl.pallas_call(
        lambda *refs: kernel(scale, *refs),
        in_specs=[smem, smem, vmem, vmem, vmem, vmem],
        out_shape=out_shape,
        scratch_shapes=[pltpu.VMEM((4 * rank, 2 * length * rows), BF16)],
        compiler_params=params(),
        name="last" if last else "step",
    )(flag, index, own, other, high, low)


def finish_kernel(flag, grads, errors, own, other, basis, new_errors, factor_q):
    rank, wide = basis.shape[0], own.shape[2]
    half = own.shape[1]
    cut = factor_q.shape[1] // 2
    first = flag[0] == 0
    top = jnp.where(first, own[...], other[...])
    low = jnp.where(first, other[...], own[...])
    a = jnp.concatenate([top[0], low[0]], axis=0)
    b = pltpu.roll(jnp.concatenate([top[1], low[1]], axis=0), cut % LANES, 1)
    whole = cut // LANES * LANES
    lane = lax.broadcasted_iota(jnp.int32, (rank, LANES), 1)
    seam = jnp.where(lane < cut % LANES, a[:, whole:], b[:, :LANES])
    q = jnp.concatenate([a[:, :whole], seam, b[:, LANES:]], axis=1)
    factor_q[...] = q
    q_high, q_low = split2(q)
    b_high, b_low = split2(basis[...].T)
    left = jnp.concatenate([b_high, b_high, b_low], axis=1)
    product = dot(left, jnp.concatenate([q_high, q_low, q_high], axis=0), NN)
    merged = grads[...].astype(F32) + errors[...].astype(F32)
    new_errors[...] = (merged - product).astype(BF16)


def finish(flag, grads, errors, own, other, basis):
    rows, width = grads.shape
    reps, half, wide = own.shape
    rank = basis.shape[0]
    block = 2 * width // reps
    cols = pl.BlockSpec((rows, block), lambda i: (0, i))
    pair = pl.BlockSpec((2, half, wide), lambda i: (i, 0, 0))
    return pl.pallas_call(
        finish_kernel,
        grid=(reps // 2,),
        in_specs=[
            pl.BlockSpec(memory_space=pltpu.SMEM),
            cols,
            cols,
            pair,
            pair,
            pl.BlockSpec((rank, rows), lambda i: (0, 0)),
        ],
        out_specs=[cols, pl.BlockSpec((rank, block), lambda i: (0, i))],
        out_shape=[jax.ShapeDtypeStruct((rows, width), BF16), jax.ShapeDtypeStruct((rank, width), F32)],
        compiler_params=params(),
        name="finish",
    )(flag, grads, errors, own, other, basis)


def exchange(chunks, axis):
    return lax.all_to_all(chunks, axis, 0, 0)


def gather(block, axis, count):
    return exchange(jnp.broadcast_to(block[None], (count,) + block.shape), axis)


def swap_cores(block):
    return lax.ppermute(block, "core", [(0, 1), (1, 0)])


def body(grads, errors, q_start):
    grads, errors = grads[0], errors[0]
    rows, width = grads.shape
    rank = q_start.shape[0]
    reps, length = lax.axis_size("rep"), lax.axis_size("z")
    core, place = lax.axis_index("core"), lax.axis_index("z")
    cut, extra = width // reps, rank // reps
    scale = 1.0 / reps
    flag = core.reshape(1).astype(jnp.int32)
    zero = jnp.zeros((1,), jnp.int32)

    block = jnp.sum(exchange(start(grads, errors, q_start, reps), "rep"), axis=0)
    own_total = lax.all_gather(block[:cut], "z")
    high, low = parts(flag, own_total, swap_cores(own_total))

    piece = block[cut : cut + extra]
    along = gather(piece, ("z", "core"), 2 * length).reshape(2 * length * extra, rows)
    left = gather(along, "rep", reps).reshape(reps, length, 2, extra, rows)
    left = left.transpose(2, 1, 0, 3, 4).reshape(2, length, rank, rows)
    own, other, order = left[0], left[1], zero
    for step in range(ITERS - 1):
        partial = iterate(scale, order, flag, own, other, high, low, False)
        own = gather(jnp.sum(exchange(partial, "rep"), axis=0), "rep", reps)
        other, order = swap_cores(own), flag
    at = (core * length + place).reshape(1).astype(jnp.int32)
    part_q, basis = iterate(scale, order, at, own, other, high, low, True)
    half = lax.dynamic_slice_in_dim(part_q, core * (rank // 2), rank // 2, 0)
    own_q = gather(half, "rep", reps)
    new_errors, factor_q = finish(flag, grads, errors, own_q, swap_cores(own_q), basis)
    return new_errors[None], factor_q


def solution(mesh):
    reps, count = mesh.devices.shape
    split = Mesh(mesh.devices.reshape(reps, count // 2, 2), ("rep", "z", "core"))
    placed = P("rep", ("z", "core"), None)
    return jax.shard_map(
        body, mesh=split, in_specs=(placed, placed, P()), out_specs=(placed, P()), check_vma=False
    )
```

```python
import functools

import jax
import jax.numpy as jnp
from jax import lax
from jax.experimental import pallas as pl
from jax.experimental.pallas import tpu as pltpu
from jax.sharding import Mesh, PartitionSpec as P

ITERS = 3
F32 = jnp.float32
BF16 = jnp.bfloat16
LANES = 128
VMEM = 20 * 1024 * 1024
SMEM_SPEC = pl.BlockSpec(memory_space=pltpu.SMEM)
VMEM_SPEC = pl.BlockSpec(memory_space=pltpu.VMEM)
HBM_SPEC = pl.BlockSpec(memory_space=pltpu.HBM)
NT = (((1,), (1,)), ((), ()))
NN = (((1,), (0,)), ((), ()))


def dot(a, b, dims):
    return lax.dot_general(a, b, dims, preferred_element_type=F32)


def split2(x):
    high = x.astype(BF16)
    return high, (x - high.astype(F32)).astype(BF16)


def split3(x):
    high = x.astype(BF16)
    rest = x - high.astype(F32)
    mid = rest.astype(BF16)
    return high, mid, (rest - mid.astype(F32)).astype(BF16)


def params(limit=VMEM):
    return pltpu.CompilerParams(vmem_limit_bytes=limit)


def start_kernel(grads, errors, q_start, out, g_held, e_held, q_held, sems):
    reps, tall, rows = out.shape
    rank, width = q_start.shape
    cut = width // reps
    extra = rank // reps
    spans = [pl.ds(2 * cut * i, 2 * cut) for i in range(reps // 2)]
    loads = []
    for i, span in enumerate(spans):
        pairs = ((grads, g_held), (errors, e_held), (q_start, q_held))
        loads.append(
            [pltpu.make_async_copy(x.at[:, span], y.at[:, span], sems.at[k, i]) for k, (x, y) in enumerate(pairs)]
        )
        for load in loads[-1]:
            load.start()
    left = jnp.zeros((2 * rank, rows), F32)
    for i, span in enumerate(spans):
        for load in loads[i]:
            load.wait()
        g, e = g_held[:, span], e_held[:, span]
        turned = (g.astype(F32) + e.astype(F32)).T
        out[2 * i, :cut, :] = turned[:cut]
        out[2 * i + 1, :cut, :] = turned[cut:]
        high, low = split2(q_held[:, span])
        both = jnp.concatenate([high, low], axis=0)
        left = left + (dot(both, g, NT) + dot(both, e, NT))
    left = left[:rank] + left[rank:]
    for i in range(reps):
        out[i, cut : cut + extra, :] = left[extra * i : extra * (i + 1)]
        out[i, cut + extra :, :] = jnp.zeros((tall - cut - extra, rows), F32)


def start(grads, errors, q_start, reps):
    rows, width = grads.shape
    tall = width // reps + 8
    return pl.pallas_call(
        start_kernel,
        in_specs=[HBM_SPEC] * 3,
        out_specs=VMEM_SPEC,
        out_shape=jax.ShapeDtypeStruct((reps, tall, rows), F32),
        scratch_shapes=[
            pltpu.VMEM(grads.shape, BF16),
            pltpu.VMEM(errors.shape, BF16),
            pltpu.VMEM(q_start.shape, F32),
            pltpu.SemaphoreType.DMA((3, reps // 2)),
        ],
        compiler_params=params(3 * VMEM),
        name="start",
    )(grads, errors, q_start)


def inverse_factor(gram_twice):
    rank, wide = gram_twice.shape
    step = 8
    count = rank // step
    row = lax.broadcasted_iota(jnp.int32, (step, wide), 0)
    col = lax.broadcasted_iota(jnp.int32, (step, wide), 1)
    a = []
    for b in range(count):
        unit = (col == row + (rank + b * step)).astype(F32)
        a.append(jnp.where(col < rank, gram_twice[b * step : (b + 1) * step], unit))

    def spread(x, k):
        return jnp.broadcast_to(x[:, k : k + 1], (step, wide))

    def line_of(x, j):
        return jnp.broadcast_to(x[j : j + 1, :], (step, wide))

    done = []
    for p in range(count):
        panel = a[p]
        f = [spread(panel, p * step + j) for j in range(step)]
        pivots = jnp.ones((step, wide), F32)
        lines, weight = [], []
        for j in range(step):
            pivot = line_of(f[j], j)
            inverse = 1.0 / pivot
            below = jnp.where(row > j, f[j], 0.0)
            line = line_of(panel, j) * inverse
            panel = panel - below * line
            ahead = {}
            for t in range(j + 1, step):
                ahead[t] = line_of(f[t], j) * inverse
                f[t] = f[t] - below * ahead[t]
            pivots = jnp.where(row == j, pivot, pivots)
            lines.append(line)
            weight.append(ahead)
        done.append(jnp.where(col < rank, 0.0, panel * lax.rsqrt(pivots)))
        for b in range(p + 1, count):
            g = [spread(a[b], p * step + j) for j in range(step)]
            for j in range(step):
                for t in range(j + 1, step):
                    g[t] = g[t] - g[j] * weight[j][t]
                a[b] = a[b] - g[j] * lines[j]
    w = jnp.concatenate(done, axis=0)
    return w + pltpu.roll(w, rank, 1)


def gram_of(held, chunk):
    rank = held.shape[0] // 4
    total = jnp.zeros((3 * rank, 4 * rank), F32)
    for at in range(0, held.shape[1], chunk):
        x = held[:, at : at + chunk]
        total = total + dot(x[: 3 * rank], x, NT)
    total = total[:rank] + (total[rank : 2 * rank] + total[2 * rank :])
    near, far = total[:, : 2 * rank], total[:, 2 * rank :]
    return near + pltpu.roll(near, rank, 1) + far


def put(held, at, x):
    rank, n = x.shape
    high, mid, low = split3(x)
    span = pl.ds(at, n)
    held[:rank, span] = high
    held[rank : 2 * rank, span] = mid
    held[2 * rank : 3 * rank, span] = low
    held[3 * rank :, span] = low


def weights(w):
    rank = w.shape[0]
    col = lax.broadcasted_iota(jnp.int32, w.shape, 1)
    once = jnp.where(col < rank, w, 0.0)
    wide = jnp.concatenate([w, once], axis=1)
    return jnp.concatenate(split3(wide), axis=0)


CHUNK = 512


def right_of(held, high, low):
    rank = held.shape[0] // 4
    cut, n = high.shape
    one = jnp.zeros((2 * rank, cut), F32)
    two = jnp.zeros((rank, cut), F32)
    for at in range(0, n, CHUNK):
        x = held[: 2 * rank, at : at + CHUNK]
        one = one + dot(x, high[:, at : at + CHUNK], NT)
        two = two + dot(x[:rank], low[:, at : at + CHUNK], NT)
    return one[:rank] + (one[rank:] + two)


def planes(info, length, mine):
    upward = info[1] == (0 if mine else 1)
    columns = 2 * LANES

    def at(j):
        plane = lax.rem(info[0] + jnp.where(upward, length - j, 1 + j), length)
        return pl.multiple_of(plane * columns, columns)

    return at


def orthonormal(info, own, other, held):
    length = own.shape[0]
    for mine, blocks in ((True, own), (False, other)):
        at = planes(info, length, mine)
        for j in range(length // 2):
            put(held, at(j), jnp.concatenate([blocks[2 * j], blocks[2 * j + 1]], axis=1))
    left = weights(inverse_factor(gram_of(held, CHUNK)))
    for at in range(0, held.shape[1], CHUNK):
        y = dot(left, held[:, at : at + CHUNK], NN)
        put(held, at, y[: y.shape[0] // 3] + (y[y.shape[0] // 3 : 2 * y.shape[0] // 3] + y[2 * y.shape[0] // 3 :]))
    return inverse_factor(gram_of(held, CHUNK))


def right_factor(scale, second, held, high, low):
    left = second[:, : second.shape[0]] * scale
    right = right_of(held, high, low)
    return jnp.dot(left, right, precision=lax.Precision.HIGHEST, preferred_element_type=F32)


def next_left(info, q, high, low, out):
    length, rank, rows = out.shape
    q_high, q_low = split2(q)
    both = jnp.concatenate([q_high, q_low], axis=0)
    at = planes(info, length, True)
    for j in range(length // 2):
        span = pl.ds(at(j), 2 * rows)
        one = dot(both, high[:, span], NN)
        x = one[:rank] + (one[rank:] + dot(q_high, low[:, span], NN))
        out[2 * j] = x[:, :rows]
        out[2 * j + 1] = x[:, rows:]


def first_kernel(scale, info, own, other, total, total_other, out, high_out, low_out, held, high, low, sems):
    length = own.shape[0]
    for mine, blocks in ((True, total), (False, total_other)):
        at = planes(info, length, mine)
        core = info[1] if mine else 1 - info[1]
        for j in range(length // 2):
            for stream in range(2):
                side = core if stream == 0 else 1 - core
                span = pl.ds(pl.multiple_of(at(j) + side * LANES, LANES), LANES)
                high[:, span], low[:, span] = split2(blocks[j, stream])
    stores = [
        pltpu.make_async_copy(high, high_out, sems.at[0]),
        pltpu.make_async_copy(low, low_out, sems.at[1]),
    ]
    for store in stores:
        store.start()
    second = orthonormal(info, own, other, held)
    next_left(info, right_factor(scale, second, held, high, low), high, low, out)
    for store in stores:
        store.wait()


def load_parts(high_in, low_in, high, low, sems):
    loads = [
        pltpu.make_async_copy(high_in, high, sems.at[0]),
        pltpu.make_async_copy(low_in, low, sems.at[1]),
    ]
    for load in loads:
        load.start()
    return loads


def step_kernel(scale, info, own, other, high_in, low_in, out, held, high, low, sems):
    loads = load_parts(high_in, low_in, high, low, sems)
    second = orthonormal(info, own, other, held)
    for load in loads:
        load.wait()
    next_left(info, right_factor(scale, second, held, high, low), high, low, out)


def last_kernel(scale, info, own, other, high_in, low_in, out, basis, held, high, low, sems):
    loads = load_parts(high_in, low_in, high, low, sems)
    length, rank, rows = own.shape
    second = orthonormal(info, own, other, held)
    for load in loads:
        load.wait()
    q = right_factor(scale, second, held, high, low)
    half = rank // 2
    quarter = half // 2
    rest = jnp.concatenate([q[:, 2 * LANES :], jnp.zeros_like(q[:, 2 * LANES :])], axis=1)
    for core in range(2):
        span = slice(core * half, (core + 1) * half)
        out[core, :half] = q[span, :LANES]
        out[core, half : 2 * half] = q[span, LANES : 2 * LANES]
        tail = rest[span]
        out[core, 2 * half :] = tail[:quarter] + pltpu.roll(tail[quarter:], LANES // 2, 1)
    at = pl.multiple_of((2 * info[0] + info[1]) * rows, rows)
    y = dot(weights(second), held[:, pl.ds(at, rows)], NN)
    basis[...] = y[:rank] + (y[rank : 2 * rank] + y[2 * rank :])


def scratch(length, rank, cut):
    n = 2 * length * LANES
    return [pltpu.VMEM((4 * rank, n), BF16)], [pltpu.VMEM((cut, n), BF16)] * 2


def first(scale, info, own, other, total, total_other):
    length, rank, rows = own.shape
    cut = total.shape[2]
    held, both = scratch(length, rank, cut)
    whole = jax.ShapeDtypeStruct((cut, 2 * length * rows), BF16)
    return pl.pallas_call(
        functools.partial(first_kernel, scale),
        in_specs=[SMEM_SPEC] + [VMEM_SPEC] * 4,
        out_specs=[VMEM_SPEC, HBM_SPEC, HBM_SPEC],
        out_shape=[jax.ShapeDtypeStruct(own.shape, F32), whole, whole],
        scratch_shapes=held + both + [pltpu.SemaphoreType.DMA((2,))],
        compiler_params=params(),
        name="first",
    )(info, own, other, total, total_other)


def step(scale, info, own, other, high, low):
    length, rank, rows = own.shape
    held, both = scratch(length, rank, high.shape[0])
    return pl.pallas_call(
        functools.partial(step_kernel, scale),
        in_specs=[SMEM_SPEC, VMEM_SPEC, VMEM_SPEC, HBM_SPEC, HBM_SPEC],
        out_shape=jax.ShapeDtypeStruct(own.shape, F32),
        scratch_shapes=held + both + [pltpu.SemaphoreType.DMA((2,))],
        compiler_params=params(),
        name="step",
    )(info, own, other, high, low)


def last(scale, info, own, other, high, low):
    length, rank, rows = own.shape
    held, both = scratch(length, rank, high.shape[0])
    shapes = [(2, 5 * rank // 4, LANES), (rank, rows)]
    return pl.pallas_call(
        functools.partial(last_kernel, scale),
        in_specs=[SMEM_SPEC, VMEM_SPEC, VMEM_SPEC, HBM_SPEC, HBM_SPEC],
        out_shape=[jax.ShapeDtypeStruct(x, F32) for x in shapes],
        scratch_shapes=held + both + [pltpu.SemaphoreType.DMA((2,))],
        compiler_params=params(),
        name="last",
    )(info, own, other, high, low)


def columns_of(top, low):
    half = top.shape[0] * 2 // 5
    quarter = half // 2
    lane = lax.broadcasted_iota(jnp.int32, (quarter, LANES), 1)
    blocks = []
    for x in (top, low):
        tail = x[2 * half :]
        upper = jnp.where(lane < LANES // 2, tail, 0.0)
        lower = jnp.where(lane < LANES // 2, pltpu.roll(tail, LANES // 2, 1), 0.0)
        blocks.append((x[:half], x[half : 2 * half], jnp.concatenate([upper, lower], axis=0)))
    return [jnp.concatenate([a, b], axis=0) for a, b in zip(*blocks)]


def finish_kernel(flag, grads, errors, own, other, basis, new_errors, factor_q):
    first_core = flag[0] == 0
    turned = basis[...].T
    b_high, b_low = split2(turned)
    left = jnp.concatenate([b_high, b_high, b_low], axis=1)
    wide = 5 * LANES
    lane = lax.broadcasted_iota(jnp.int32, (basis.shape[0], LANES), 1)
    for i in range(own.shape[0] // 2):
        even, odd = [
            columns_of(jnp.where(first_core, own[j], other[j]), jnp.where(first_core, other[j], own[j]))
            for j in (2 * i, 2 * i + 1)
        ]
        turn = [pltpu.roll(x, LANES // 2, 1) for x in odd]
        low_lane = lane < LANES // 2
        q = jnp.concatenate(
            [
                even[0],
                even[1],
                jnp.where(low_lane, even[2], turn[0]),
                jnp.where(low_lane, turn[0], turn[1]),
                jnp.where(low_lane, turn[1], turn[2]),
            ],
            axis=1,
        )
        span = slice(i * wide, (i + 1) * wide)
        factor_q[:, span] = q
        q_high, q_low = split2(q)
        product = dot(left, jnp.concatenate([q_high, q_low, q_high], axis=0), NN)
        merged = grads[:, span].astype(F32) + errors[:, span].astype(F32)
        new_errors[:, span] = (merged - product).astype(BF16)


def finish(flag, grads, errors, own, other, basis):
    rows, width = grads.shape
    reps, tall, lanes = own.shape
    rank = basis.shape[0]
    steps = 4
    cols = pl.BlockSpec((rows, width // steps), lambda i: (0, i))
    piece = pl.BlockSpec((reps // steps, tall, lanes), lambda i: (i, 0, 0))
    return pl.pallas_call(
        finish_kernel,
        grid=(steps,),
        in_specs=[SMEM_SPEC, cols, cols, piece, piece, pl.BlockSpec((rank, rows), lambda i: (0, 0))],
        out_specs=[cols, pl.BlockSpec((rank, width // steps), lambda i: (0, i))],
        out_shape=[jax.ShapeDtypeStruct((rows, width), BF16), jax.ShapeDtypeStruct((rank, width), F32)],
        compiler_params=params(),
        name="finish",
    )(flag, grads, errors, own, other, basis)


def exchange(chunks, axis):
    return lax.all_to_all(chunks, axis, 0, 0)


def gather(block, axis, count):
    return exchange(jnp.broadcast_to(block[None], (count,) + block.shape), axis)


def swap_cores(block):
    return lax.ppermute(block, "core", [(0, 1), (1, 0)])


def ring(block, length):
    half = length // 2
    up = [(2 * i, 2 * ((i + 1) % length)) for i in range(length)]
    down = [(2 * i + 1, 2 * ((i - 1) % length) + 1) for i in range(length)]
    blocks = [block]
    for s in range(half):
        blocks.append(lax.ppermute(blocks[-1], ("z", "core"), up + down if s < half - 1 else down))
    return blocks


def body(grads, errors, q_start):
    grads, errors = grads[0], errors[0]
    rows, width = grads.shape
    rank = q_start.shape[0]
    reps, length = lax.axis_size("rep"), lax.axis_size("z")
    core, place = lax.axis_index("core"), lax.axis_index("z")
    cut, extra = width // reps, rank // reps
    scale = 1.0 / reps
    flag = core.reshape(1).astype(jnp.int32)
    info = jnp.stack([place, core]).astype(jnp.int32)

    block = jnp.sum(exchange(start(grads, errors, q_start, reps), "rep"), axis=0)
    streams = ring(block, length), ring(swap_cores(block), length)
    held = jnp.stack(
        [jnp.stack([jnp.where(core == 0, x[j], x[j + 1]) for x in streams]) for j in range(length // 2)]
    )
    total = held[:, :, :cut]
    piece = held[:, :, cut : cut + extra]
    piece = jnp.where(core == 0, piece, piece[:, ::-1]).reshape(length * extra, rows)
    own = gather(piece, "rep", reps).reshape(reps, length, extra, rows)
    own = own.transpose(1, 0, 2, 3).reshape(length, rank, rows)
    partial, high, low = first(scale, info, own, swap_cores(own), total, swap_cores(total))
    for turn in range(ITERS - 1):
        own = gather(jnp.sum(exchange(partial, "rep"), axis=0), "rep", reps)
        if turn < ITERS - 2:
            partial = step(scale, info, own, swap_cores(own), high, low)
    part_q, basis = last(scale, info, own, swap_cores(own), high, low)
    own_q = gather(lax.dynamic_index_in_dim(part_q, core, 0, False), "rep", reps)
    new_errors, factor_q = finish(flag, grads, errors, own_q, swap_cores(own_q), basis)
    return new_errors[None], factor_q


def solution(mesh):
    reps, count = mesh.devices.shape
    split = Mesh(mesh.devices.reshape(reps, count // 2, 2), ("rep", "z", "core"))
    placed = P("rep", ("z", "core"), None)
    return jax.shard_map(
        body, mesh=split, in_specs=(placed, placed, P()), out_specs=(placed, P()), check_vma=False
    )
```

```python
import functools

import jax
import jax.numpy as jnp
from jax import lax
from jax.experimental import pallas as pl
from jax.experimental.pallas import tpu as pltpu
from jax.sharding import Mesh, PartitionSpec as P

ITERS = 3
F32 = jnp.float32
BF16 = jnp.bfloat16
LANES = 128
VMEM = 20 * 1024 * 1024
SMEM_SPEC = pl.BlockSpec(memory_space=pltpu.SMEM)
VMEM_SPEC = pl.BlockSpec(memory_space=pltpu.VMEM)
HBM_SPEC = pl.BlockSpec(memory_space=pltpu.HBM)
NT = (((1,), (1,)), ((), ()))
NN = (((1,), (0,)), ((), ()))


def dot(a, b, dims):
    return lax.dot_general(a, b, dims, preferred_element_type=F32)


def split2(x):
    high = x.astype(BF16)
    return high, (x - high.astype(F32)).astype(BF16)


def split3(x):
    high = x.astype(BF16)
    rest = x - high.astype(F32)
    mid = rest.astype(BF16)
    return high, mid, (rest - mid.astype(F32)).astype(BF16)


def params(limit=VMEM):
    return pltpu.CompilerParams(vmem_limit_bytes=limit)


def start_kernel(grads, errors, q_start, near, far, g_held, e_held, q_held, sems):
    reps, tall, rows = near.shape
    split = tall - 8
    rank, width = q_start.shape
    cut = width // reps
    extra = rank // reps
    spans = [pl.ds(2 * cut * i, 2 * cut) for i in range(reps // 2)]
    loads = []
    for i, span in enumerate(spans):
        pairs = ((grads, g_held), (errors, e_held), (q_start, q_held))
        loads.append(
            [pltpu.make_async_copy(x.at[:, span], y.at[:, span], sems.at[k, i]) for k, (x, y) in enumerate(pairs)]
        )
        for load in loads[-1]:
            load.start()
    left = jnp.zeros((2 * rank, rows), F32)
    for i, span in enumerate(spans):
        for load in loads[i]:
            load.wait()
        g, e = g_held[:, span], e_held[:, span]
        turned = (g.astype(F32) + e.astype(F32)).T
        for side in range(2):
            near[2 * i + side, :split, :] = turned[side * cut : side * cut + split]
            far[2 * i + side] = turned[side * cut + split : (side + 1) * cut]
        high, low = split2(q_held[:, span])
        both = jnp.concatenate([high, low], axis=0)
        left = left + (dot(both, g, NT) + dot(both, e, NT))
    left = left[:rank] + left[rank:]
    for i in range(reps):
        near[i, split : split + extra, :] = left[extra * i : extra * (i + 1)]
        near[i, split + extra :, :] = jnp.zeros((tall - split - extra, rows), F32)


def start(grads, errors, q_start, reps, split):
    rows, width = grads.shape
    rest = width // reps - split
    return pl.pallas_call(
        start_kernel,
        in_specs=[HBM_SPEC] * 3,
        out_specs=[VMEM_SPEC, VMEM_SPEC],
        out_shape=[jax.ShapeDtypeStruct((reps, tall, rows), F32) for tall in (split + 8, rest)],
        scratch_shapes=[
            pltpu.VMEM(grads.shape, BF16),
            pltpu.VMEM(errors.shape, BF16),
            pltpu.VMEM(q_start.shape, F32),
            pltpu.SemaphoreType.DMA((3, reps // 2)),
        ],
        compiler_params=params(3 * VMEM),
        name="start",
    )(grads, errors, q_start)


def inverse_factor(gram_twice):
    rank, wide = gram_twice.shape
    step = 8
    count = rank // step
    row = lax.broadcasted_iota(jnp.int32, (step, wide), 0)
    col = lax.broadcasted_iota(jnp.int32, (step, wide), 1)
    a = []
    for b in range(count):
        unit = (col == row + (rank + b * step)).astype(F32)
        a.append(jnp.where(col < rank, gram_twice[b * step : (b + 1) * step], unit))

    def spread(x, k):
        return jnp.broadcast_to(x[:, k : k + 1], (step, wide))

    def line_of(x, j):
        return jnp.broadcast_to(x[j : j + 1, :], (step, wide))

    done = []
    for p in range(count):
        panel = a[p]
        f = [spread(panel, p * step + j) for j in range(step)]
        pivots = jnp.ones((step, wide), F32)
        lines, weight = [], []
        for j in range(step):
            pivot = line_of(f[j], j)
            inverse = 1.0 / pivot
            below = jnp.where(row > j, f[j], 0.0)
            line = line_of(panel, j) * inverse
            panel = panel - below * line
            ahead = {}
            for t in range(j + 1, step):
                ahead[t] = line_of(f[t], j) * inverse
                f[t] = f[t] - below * ahead[t]
            pivots = jnp.where(row == j, pivot, pivots)
            lines.append(line)
            weight.append(ahead)
        done.append(jnp.where(col < rank, 0.0, panel * lax.rsqrt(pivots)))
        for b in range(p + 1, count):
            g = [spread(a[b], p * step + j) for j in range(step)]
            for j in range(step):
                for t in range(j + 1, step):
                    g[t] = g[t] - g[j] * weight[j][t]
                a[b] = a[b] - g[j] * lines[j]
    w = jnp.concatenate(done, axis=0)
    return w + pltpu.roll(w, rank, 1)


def gram_of(held, chunk):
    rank = held.shape[0] // 4
    total = jnp.zeros((3 * rank, 4 * rank), F32)
    for at in range(0, held.shape[1], chunk):
        x = held[:, at : at + chunk]
        total = total + dot(x[: 3 * rank], x, NT)
    total = total[:rank] + (total[rank : 2 * rank] + total[2 * rank :])
    near, far = total[:, : 2 * rank], total[:, 2 * rank :]
    return near + pltpu.roll(near, rank, 1) + far


def put(held, at, x):
    rank, n = x.shape
    high, mid, low = split3(x)
    span = pl.ds(at, n)
    held[:rank, span] = high
    held[rank : 2 * rank, span] = mid
    held[2 * rank : 3 * rank, span] = low
    held[3 * rank :, span] = low


def weights(w):
    rank = w.shape[0]
    col = lax.broadcasted_iota(jnp.int32, w.shape, 1)
    once = jnp.where(col < rank, w, 0.0)
    wide = jnp.concatenate([w, once], axis=1)
    return jnp.concatenate(split3(wide), axis=0)


CHUNK = 512


def right_of(held, high, low):
    rank = held.shape[0] // 4
    cut, n = high.shape
    one = jnp.zeros((2 * rank, cut), F32)
    two = jnp.zeros((rank, cut), F32)
    for at in range(0, n, CHUNK):
        x = held[: 2 * rank, at : at + CHUNK]
        one = one + dot(x, high[:, at : at + CHUNK], NT)
        two = two + dot(x[:rank], low[:, at : at + CHUNK], NT)
    return one[:rank] + (one[rank:] + two)


def planes(info, length, mine):
    upward = info[1] == (0 if mine else 1)
    columns = 2 * LANES

    def at(j):
        plane = lax.rem(info[0] + jnp.where(upward, length - j, 1 + j), length)
        return pl.multiple_of(plane * columns, columns)

    return at


def orthonormal(info, own, other, held):
    length = own.shape[0]
    for mine, blocks in ((True, own), (False, other)):
        at = planes(info, length, mine)
        for j in range(length // 2):
            put(held, at(j), jnp.concatenate([blocks[2 * j], blocks[2 * j + 1]], axis=1))
    left = weights(inverse_factor(gram_of(held, CHUNK)))
    for at in range(0, held.shape[1], CHUNK):
        y = dot(left, held[:, at : at + CHUNK], NN)
        put(held, at, y[: y.shape[0] // 3] + (y[y.shape[0] // 3 : 2 * y.shape[0] // 3] + y[2 * y.shape[0] // 3 :]))
    return inverse_factor(gram_of(held, CHUNK))


def right_factor(scale, second, held, high, low):
    left = second[:, : second.shape[0]] * scale
    right = right_of(held, high, low)
    return jnp.dot(left, right, precision=lax.Precision.HIGHEST, preferred_element_type=F32)


def next_left(info, q, high, low, out):
    length, rank, rows = out.shape
    q_high, q_low = split2(q)
    both = jnp.concatenate([q_high, q_low], axis=0)
    at = planes(info, length, True)
    for j in range(length // 2):
        span = pl.ds(at(j), 2 * rows)
        one = dot(both, high[:, span], NN)
        x = one[:rank] + (one[rank:] + dot(q_high, low[:, span], NN))
        out[2 * j] = x[:, :rows]
        out[2 * j + 1] = x[:, rows:]


def orth_kernel(info, own, other, rows_out, weights_out, held):
    weights_out[...] = orthonormal(info, own, other, held)
    rows_out[...] = held[...]


def first_kernel(scale, info, held, second, near, near_other, far, far_other, out, high_out, low_out, high, low, sems):
    length = out.shape[0]
    split = near.shape[2]
    for mine, pieces in ((True, (near, far)), (False, (near_other, far_other))):
        at = planes(info, length, mine)
        core = info[1] if mine else 1 - info[1]
        for j in range(length // 2):
            for stream in range(2):
                side = core if stream == 0 else 1 - core
                span = pl.ds(pl.multiple_of(at(j) + side * LANES, LANES), LANES)
                for blocks, rows in zip(pieces, (slice(0, split), slice(split, high.shape[0]))):
                    high[rows, span], low[rows, span] = split2(blocks[j, stream])
    stores = [
        pltpu.make_async_copy(high, high_out, sems.at[0]),
        pltpu.make_async_copy(low, low_out, sems.at[1]),
    ]
    for store in stores:
        store.start()
    next_left(info, right_factor(scale, second[...], held, high, low), high, low, out)
    for store in stores:
        store.wait()


def load_parts(high_in, low_in, high, low, sems):
    loads = [
        pltpu.make_async_copy(high_in, high, sems.at[0]),
        pltpu.make_async_copy(low_in, low, sems.at[1]),
    ]
    for load in loads:
        load.start()
    return loads


def step_kernel(scale, info, own, other, high_in, low_in, out, held, high, low, sems):
    loads = load_parts(high_in, low_in, high, low, sems)
    second = orthonormal(info, own, other, held)
    for load in loads:
        load.wait()
    next_left(info, right_factor(scale, second, held, high, low), high, low, out)


def last_kernel(scale, info, own, other, high_in, low_in, out, basis, held, high, low, sems):
    loads = load_parts(high_in, low_in, high, low, sems)
    length, rank, rows = own.shape
    second = orthonormal(info, own, other, held)
    for load in loads:
        load.wait()
    q = right_factor(scale, second, held, high, low)
    half = rank // 2
    quarter = half // 2
    rest = jnp.concatenate([q[:, 2 * LANES :], jnp.zeros_like(q[:, 2 * LANES :])], axis=1)
    for core in range(2):
        span = slice(core * half, (core + 1) * half)
        out[core, :half] = q[span, :LANES]
        out[core, half : 2 * half] = q[span, LANES : 2 * LANES]
        tail = rest[span]
        out[core, 2 * half :] = tail[:quarter] + pltpu.roll(tail[quarter:], LANES // 2, 1)
    at = pl.multiple_of((2 * info[0] + info[1]) * rows, rows)
    y = dot(weights(second), held[:, pl.ds(at, rows)], NN)
    basis[...] = y[:rank] + (y[rank : 2 * rank] + y[2 * rank :])


def scratch(length, rank, cut):
    n = 2 * length * LANES
    return [pltpu.VMEM((4 * rank, n), BF16)], [pltpu.VMEM((cut, n), BF16)] * 2


def orth(info, own, other):
    length, rank, rows = own.shape
    shape = (4 * rank, 2 * length * rows)
    return pl.pallas_call(
        orth_kernel,
        in_specs=[SMEM_SPEC, VMEM_SPEC, VMEM_SPEC],
        out_shape=[jax.ShapeDtypeStruct(shape, BF16), jax.ShapeDtypeStruct((rank, 2 * rank), F32)],
        scratch_shapes=[pltpu.VMEM(shape, BF16)],
        compiler_params=params(),
        name="orth",
    )(info, own, other)


def first(scale, info, held, second, near, far, shape):
    length, rank, rows = shape
    cut = near[0].shape[2] + far[0].shape[2]
    _, both = scratch(length, rank, cut)
    whole = jax.ShapeDtypeStruct((cut, 2 * length * rows), BF16)
    return pl.pallas_call(
        functools.partial(first_kernel, scale),
        in_specs=[SMEM_SPEC] + [VMEM_SPEC] * 6,
        out_specs=[VMEM_SPEC, HBM_SPEC, HBM_SPEC],
        out_shape=[jax.ShapeDtypeStruct(shape, F32), whole, whole],
        scratch_shapes=both + [pltpu.SemaphoreType.DMA((2,))],
        compiler_params=params(),
        name="first",
    )(info, held, second, *near, *far)


def step(scale, info, own, other, high, low):
    length, rank, rows = own.shape
    held, both = scratch(length, rank, high.shape[0])
    return pl.pallas_call(
        functools.partial(step_kernel, scale),
        in_specs=[SMEM_SPEC, VMEM_SPEC, VMEM_SPEC, HBM_SPEC, HBM_SPEC],
        out_shape=jax.ShapeDtypeStruct(own.shape, F32),
        scratch_shapes=held + both + [pltpu.SemaphoreType.DMA((2,))],
        compiler_params=params(),
        name="step",
    )(info, own, other, high, low)


def last(scale, info, own, other, high, low):
    length, rank, rows = own.shape
    held, both = scratch(length, rank, high.shape[0])
    shapes = [(2, 5 * rank // 4, LANES), (rank, rows)]
    return pl.pallas_call(
        functools.partial(last_kernel, scale),
        in_specs=[SMEM_SPEC, VMEM_SPEC, VMEM_SPEC, HBM_SPEC, HBM_SPEC],
        out_shape=[jax.ShapeDtypeStruct(x, F32) for x in shapes],
        scratch_shapes=held + both + [pltpu.SemaphoreType.DMA((2,))],
        compiler_params=params(),
        name="last",
    )(info, own, other, high, low)


def columns_of(top, low):
    half = top.shape[0] * 2 // 5
    quarter = half // 2
    lane = lax.broadcasted_iota(jnp.int32, (quarter, LANES), 1)
    blocks = []
    for x in (top, low):
        tail = x[2 * half :]
        upper = jnp.where(lane < LANES // 2, tail, 0.0)
        lower = jnp.where(lane < LANES // 2, pltpu.roll(tail, LANES // 2, 1), 0.0)
        blocks.append((x[:half], x[half : 2 * half], jnp.concatenate([upper, lower], axis=0)))
    return [jnp.concatenate([a, b], axis=0) for a, b in zip(*blocks)]


def finish_kernel(flag, grads, errors, own, other, basis, new_errors, factor_q):
    first_core = flag[0] == 0
    turned = basis[...].T
    b_high, b_low = split2(turned)
    left = jnp.concatenate([b_high, b_high, b_low], axis=1)
    wide = 5 * LANES
    lane = lax.broadcasted_iota(jnp.int32, (basis.shape[0], LANES), 1)
    for i in range(own.shape[0] // 2):
        even, odd = [
            columns_of(jnp.where(first_core, own[j], other[j]), jnp.where(first_core, other[j], own[j]))
            for j in (2 * i, 2 * i + 1)
        ]
        turn = [pltpu.roll(x, LANES // 2, 1) for x in odd]
        low_lane = lane < LANES // 2
        q = jnp.concatenate(
            [
                even[0],
                even[1],
                jnp.where(low_lane, even[2], turn[0]),
                jnp.where(low_lane, turn[0], turn[1]),
                jnp.where(low_lane, turn[1], turn[2]),
            ],
            axis=1,
        )
        span = slice(i * wide, (i + 1) * wide)
        factor_q[:, span] = q
        q_high, q_low = split2(q)
        product = dot(left, jnp.concatenate([q_high, q_low, q_high], axis=0), NN)
        merged = grads[:, span].astype(F32) + errors[:, span].astype(F32)
        new_errors[:, span] = (merged - product).astype(BF16)


def finish(flag, grads, errors, own, other, basis):
    rows, width = grads.shape
    reps, tall, lanes = own.shape
    rank = basis.shape[0]
    steps = 4
    cols = pl.BlockSpec((rows, width // steps), lambda i: (0, i))
    piece = pl.BlockSpec((reps // steps, tall, lanes), lambda i: (i, 0, 0))
    return pl.pallas_call(
        finish_kernel,
        grid=(steps,),
        in_specs=[SMEM_SPEC, cols, cols, piece, piece, pl.BlockSpec((rank, rows), lambda i: (0, 0))],
        out_specs=[cols, pl.BlockSpec((rank, width // steps), lambda i: (0, i))],
        out_shape=[jax.ShapeDtypeStruct((rows, width), BF16), jax.ShapeDtypeStruct((rank, width), F32)],
        compiler_params=params(),
        name="finish",
    )(flag, grads, errors, own, other, basis)


def exchange(chunks, axis):
    return lax.all_to_all(chunks, axis, 0, 0)


def gather(block, axis, count):
    return exchange(jnp.broadcast_to(block[None], (count,) + block.shape), axis)


def swap_cores(block):
    return lax.ppermute(block, "core", [(0, 1), (1, 0)])


def ring_step(block, length, both):
    up = [(2 * i, 2 * ((i + 1) % length)) for i in range(length)]
    down = [(2 * i + 1, 2 * ((i - 1) % length) + 1) for i in range(length)]
    return lax.ppermute(block, ("z", "core"), up + down if both else down)


def after(x, earlier):
    return lax.optimization_barrier((x, earlier))[0]


LAG = 1


def body(grads, errors, q_start):
    grads, errors = grads[0], errors[0]
    rows, width = grads.shape
    rank = q_start.shape[0]
    reps, length = lax.axis_size("rep"), lax.axis_size("z")
    core, place = lax.axis_index("core"), lax.axis_index("z")
    cut, extra = width // reps, rank // reps
    split = cut // 2
    half = length // 2
    scale = 1.0 / reps
    flag = core.reshape(1).astype(jnp.int32)
    info = jnp.stack([place, core]).astype(jnp.int32)

    def pair(block):
        return jnp.stack([block, swap_cores(block)])

    near, far = start(grads, errors, q_start, reps, split)
    near = jnp.sum(exchange(near, "rep"), axis=0)
    far = jnp.sum(exchange(after(far, near), "rep"), axis=0)
    rings = [[pair(near)], []]
    for turn in range(half + LAG):
        if turn == LAG:
            rings[1].append(pair(after(far, rings[0][-1])))
        for blocks in rings:
            s = len(blocks)
            if 0 < s <= half:
                blocks.append(ring_step(blocks[-1], length, s < half))
    def stacked(blocks):
        return jnp.stack([jnp.where(core == 0, blocks[j], blocks[j + 1]) for j in range(half)])

    near = stacked(rings[0])
    piece = near[:, :, split : split + extra]
    near = near[:, :, :split]
    piece = jnp.where(core == 0, piece, piece[:, ::-1]).reshape(length * extra, rows)
    own = gather(piece, "rep", reps).reshape(reps, length, extra, rows)
    own = own.transpose(1, 0, 2, 3).reshape(length, rank, rows)
    rings[1][-1] = after(rings[1][-1], own)
    far = stacked(rings[1])
    held, weight = orth(info, own, swap_cores(own))
    partial, high, low = first(
        scale, info, held, weight, (near, swap_cores(near)), (far, swap_cores(far)), own.shape
    )
    for turn in range(ITERS - 1):
        own = gather(jnp.sum(exchange(partial, "rep"), axis=0), "rep", reps)
        if turn < ITERS - 2:
            partial = step(scale, info, own, swap_cores(own), high, low)
    part_q, basis = last(scale, info, own, swap_cores(own), high, low)
    own_q = gather(lax.dynamic_index_in_dim(part_q, core, 0, False), "rep", reps)
    new_errors, factor_q = finish(flag, grads, errors, own_q, swap_cores(own_q), basis)
    return new_errors[None], factor_q


def solution(mesh):
    reps, count = mesh.devices.shape
    split = Mesh(mesh.devices.reshape(reps, count // 2, 2), ("rep", "z", "core"))
    placed = P("rep", ("z", "core"), None)
    return jax.shard_map(
        body, mesh=split, in_specs=(placed, placed, P()), out_specs=(placed, P()), check_vma=False
    )
```

```python
import functools

import jax
import jax.numpy as jnp
from jax import lax
from jax.experimental import pallas as pl
from jax.experimental.pallas import tpu as pltpu
from jax.sharding import Mesh, PartitionSpec as P

ITERS = 3
F32 = jnp.float32
BF16 = jnp.bfloat16
LANES = 128
VMEM = 20 * 1024 * 1024
WIDE = 58 * 1024 * 1024
SMEM_SPEC = pl.BlockSpec(memory_space=pltpu.SMEM)
VMEM_SPEC = pl.BlockSpec(memory_space=pltpu.VMEM)
HBM_SPEC = pl.BlockSpec(memory_space=pltpu.HBM)
NT = (((1,), (1,)), ((), ()))
NN = (((1,), (0,)), ((), ()))


def dot(a, b, dims):
    return lax.dot_general(a, b, dims, preferred_element_type=F32)


def split2(x):
    high = x.astype(BF16)
    return high, (x - high.astype(F32)).astype(BF16)


def split3(x):
    high = x.astype(BF16)
    rest = x - high.astype(F32)
    mid = rest.astype(BF16)
    return high, mid, (rest - mid.astype(F32)).astype(BF16)


def params(limit=VMEM):
    return pltpu.CompilerParams(vmem_limit_bytes=limit)


def start_kernel(grads, errors, q_start, out, g_held, e_held, q_held, sems):
    reps, tall, rows = out.shape
    rank, width = q_start.shape
    cut = width // reps
    extra = rank // reps
    spans = [pl.ds(2 * cut * i, 2 * cut) for i in range(reps // 2)]
    loads = []
    for i, span in enumerate(spans):
        pairs = ((grads, g_held), (errors, e_held), (q_start, q_held))
        loads.append(
            [pltpu.make_async_copy(x.at[:, span], y.at[:, span], sems.at[k, i]) for k, (x, y) in enumerate(pairs)]
        )
        for load in loads[-1]:
            load.start()
    left = jnp.zeros((2 * rank, rows), F32)
    for i, span in enumerate(spans):
        for load in loads[i]:
            load.wait()
        g, e = g_held[:, span], e_held[:, span]
        turned = (g.astype(F32) + e.astype(F32)).T
        out[2 * i, :cut, :] = turned[:cut]
        out[2 * i + 1, :cut, :] = turned[cut:]
        high, low = split2(q_held[:, span])
        both = jnp.concatenate([high, low], axis=0)
        left = left + (dot(both, g, NT) + dot(both, e, NT))
    left = left[:rank] + left[rank:]
    for i in range(reps):
        out[i, cut : cut + extra, :] = left[extra * i : extra * (i + 1)]
        out[i, cut + extra :, :] = jnp.zeros((tall - cut - extra, rows), F32)


def start(grads, errors, q_start, reps):
    rows, width = grads.shape
    tall = width // reps + 8
    return pl.pallas_call(
        start_kernel,
        in_specs=[HBM_SPEC] * 3,
        out_specs=VMEM_SPEC,
        out_shape=jax.ShapeDtypeStruct((reps, tall, rows), F32),
        scratch_shapes=[
            pltpu.VMEM(grads.shape, BF16),
            pltpu.VMEM(errors.shape, BF16),
            pltpu.VMEM(q_start.shape, F32),
            pltpu.SemaphoreType.DMA((3, reps // 2)),
        ],
        compiler_params=params(3 * VMEM),
        name="start",
    )(grads, errors, q_start)


def inverse_factor(gram_twice):
    rank, wide = gram_twice.shape
    step = 8
    count = rank // step
    row = lax.broadcasted_iota(jnp.int32, (step, wide), 0)
    col = lax.broadcasted_iota(jnp.int32, (step, wide), 1)
    a = []
    for b in range(count):
        unit = (col == row + (rank + b * step)).astype(F32)
        a.append(jnp.where(col < rank, gram_twice[b * step : (b + 1) * step], unit))

    def spread(x, k):
        return jnp.broadcast_to(x[:, k : k + 1], (step, wide))

    def line_of(x, j):
        return jnp.broadcast_to(x[j : j + 1, :], (step, wide))

    done = []
    for p in range(count):
        panel = a[p]
        f = [spread(panel, p * step + j) for j in range(step)]
        pivots = jnp.ones((step, wide), F32)
        lines, weight = [], []
        for j in range(step):
            pivot = line_of(f[j], j)
            inverse = 1.0 / pivot
            below = jnp.where(row > j, f[j], 0.0)
            line = line_of(panel, j) * inverse
            panel = panel - below * line
            ahead = {}
            for t in range(j + 1, step):
                ahead[t] = line_of(f[t], j) * inverse
                f[t] = f[t] - below * ahead[t]
            pivots = jnp.where(row == j, pivot, pivots)
            lines.append(line)
            weight.append(ahead)
        done.append(jnp.where(col < rank, 0.0, panel * lax.rsqrt(pivots)))
        for b in range(p + 1, count):
            g = [spread(a[b], p * step + j) for j in range(step)]
            for j in range(step):
                for t in range(j + 1, step):
                    g[t] = g[t] - g[j] * weight[j][t]
                a[b] = a[b] - g[j] * lines[j]
    w = jnp.concatenate(done, axis=0)
    return w + pltpu.roll(w, rank, 1)


def gram_of(held, chunk):
    rank = held.shape[0] // 4
    total = jnp.zeros((3 * rank, 4 * rank), F32)
    for at in range(0, held.shape[1], chunk):
        x = held[:, at : at + chunk]
        total = total + dot(x[: 3 * rank], x, NT)
    total = total[:rank] + (total[rank : 2 * rank] + total[2 * rank :])
    near, far = total[:, : 2 * rank], total[:, 2 * rank :]
    return near + pltpu.roll(near, rank, 1) + far


def put(held, at, x):
    rank, n = x.shape
    high, mid, low = split3(x)
    span = pl.ds(at, n)
    held[:rank, span] = high
    held[rank : 2 * rank, span] = mid
    held[2 * rank : 3 * rank, span] = low
    held[3 * rank :, span] = low


def weights(w):
    rank = w.shape[0]
    col = lax.broadcasted_iota(jnp.int32, w.shape, 1)
    once = jnp.where(col < rank, w, 0.0)
    wide = jnp.concatenate([w, once], axis=1)
    return jnp.concatenate(split3(wide), axis=0)


CHUNK = 512


def right_of(held, high, low):
    rank = held.shape[0] // 4
    cut, n = high.shape
    one = jnp.zeros((2 * rank, cut), F32)
    two = jnp.zeros((rank, cut), F32)
    for at in range(0, n, CHUNK):
        x = held[: 2 * rank, at : at + CHUNK]
        one = one + dot(x, high[:, at : at + CHUNK], NT)
        two = two + dot(x[:rank], low[:, at : at + CHUNK], NT)
    return one[:rank] + (one[rank:] + two)


def planes(info, length, mine):
    upward = info[1] == (0 if mine else 1)
    columns = 2 * LANES

    def at(j):
        plane = lax.rem(info[0] + jnp.where(upward, length - j, 1 + j), length)
        return pl.multiple_of(plane * columns, columns)

    return at


def orthonormal(info, own, other, held):
    length = own.shape[0]
    for mine, blocks in ((True, own), (False, other)):
        at = planes(info, length, mine)
        for j in range(length // 2):
            put(held, at(j), jnp.concatenate([blocks[2 * j], blocks[2 * j + 1]], axis=1))
    left = weights(inverse_factor(gram_of(held, CHUNK)))
    for at in range(0, held.shape[1], CHUNK):
        y = dot(left, held[:, at : at + CHUNK], NN)
        put(held, at, y[: y.shape[0] // 3] + (y[y.shape[0] // 3 : 2 * y.shape[0] // 3] + y[2 * y.shape[0] // 3 :]))
    return inverse_factor(gram_of(held, CHUNK))


def right_factor(scale, second, held, high, low):
    left = second[:, : second.shape[0]] * scale
    right = right_of(held, high, low)
    return jnp.dot(left, right, precision=lax.Precision.HIGHEST, preferred_element_type=F32)


def next_left(info, q, high, low, out):
    length, rank, rows = out.shape
    q_high, q_low = split2(q)
    both = jnp.concatenate([q_high, q_low], axis=0)
    at = planes(info, length, True)
    for j in range(length // 2):
        span = pl.ds(at(j), 2 * rows)
        one = dot(both, high[:, span], NN)
        x = one[:rank] + (one[rank:] + dot(q_high, low[:, span], NN))
        out[2 * j] = x[:, :rows]
        out[2 * j + 1] = x[:, rows:]


def first_kernel(scale, info, own, other, total, total_other, out, high_out, low_out, held, high, low, sems):
    length = own.shape[0]
    for mine, blocks in ((True, total), (False, total_other)):
        at = planes(info, length, mine)
        core = info[1] if mine else 1 - info[1]
        for j in range(length // 2):
            for stream in range(2):
                side = core if stream == 0 else 1 - core
                span = pl.ds(pl.multiple_of(at(j) + side * LANES, LANES), LANES)
                high[:, span], low[:, span] = split2(blocks[j, stream])
    stores = [
        pltpu.make_async_copy(high, high_out, sems.at[0]),
        pltpu.make_async_copy(low, low_out, sems.at[1]),
    ]
    for store in stores:
        store.start()
    second = orthonormal(info, own, other, held)
    next_left(info, right_factor(scale, second, held, high, low), high, low, out)
    for store in stores:
        store.wait()


def load_parts(high_in, low_in, high, low, sems):
    loads = [
        pltpu.make_async_copy(high_in, high, sems.at[0]),
        pltpu.make_async_copy(low_in, low, sems.at[1]),
    ]
    for load in loads:
        load.start()
    return loads


def step_kernel(scale, info, own, other, high_in, low_in, out, held, high, low, sems):
    loads = load_parts(high_in, low_in, high, low, sems)
    second = orthonormal(info, own, other, held)
    for load in loads:
        load.wait()
    next_left(info, right_factor(scale, second, held, high, low), high, low, out)


def last_kernel(scale, info, own, other, high_in, low_in, out, basis, held, high, low, sems):
    loads = load_parts(high_in, low_in, high, low, sems)
    length, rank, rows = own.shape
    second = orthonormal(info, own, other, held)
    for load in loads:
        load.wait()
    q = right_factor(scale, second, held, high, low)
    half = rank // 2
    quarter = half // 2
    rest = jnp.concatenate([q[:, 2 * LANES :], jnp.zeros_like(q[:, 2 * LANES :])], axis=1)
    for core in range(2):
        span = slice(core * half, (core + 1) * half)
        out[core, :half] = q[span, :LANES]
        out[core, half : 2 * half] = q[span, LANES : 2 * LANES]
        tail = rest[span]
        out[core, 2 * half :] = tail[:quarter] + pltpu.roll(tail[quarter:], LANES // 2, 1)
    at = pl.multiple_of((2 * info[0] + info[1]) * rows, rows)
    y = dot(weights(second), held[:, pl.ds(at, rows)], NN)
    basis[...] = y[:rank] + (y[rank : 2 * rank] + y[2 * rank :])


def scratch(length, rank, cut):
    n = 2 * length * LANES
    return [pltpu.VMEM((4 * rank, n), BF16)], [pltpu.VMEM((cut, n), BF16)] * 2


def first(scale, info, own, other, total, total_other):
    length, rank, rows = own.shape
    cut = total.shape[2]
    held, both = scratch(length, rank, cut)
    whole = jax.ShapeDtypeStruct((cut, 2 * length * rows), BF16)
    return pl.pallas_call(
        functools.partial(first_kernel, scale),
        in_specs=[SMEM_SPEC] + [VMEM_SPEC] * 4,
        out_specs=[VMEM_SPEC, HBM_SPEC, HBM_SPEC],
        out_shape=[jax.ShapeDtypeStruct(own.shape, F32), whole, whole],
        scratch_shapes=held + both + [pltpu.SemaphoreType.DMA((2,))],
        compiler_params=params(),
        name="first",
    )(info, own, other, total, total_other)


def step(scale, info, own, other, high, low):
    length, rank, rows = own.shape
    held, both = scratch(length, rank, high.shape[0])
    return pl.pallas_call(
        functools.partial(step_kernel, scale),
        in_specs=[SMEM_SPEC, VMEM_SPEC, VMEM_SPEC, HBM_SPEC, HBM_SPEC],
        out_shape=jax.ShapeDtypeStruct(own.shape, F32),
        scratch_shapes=held + both + [pltpu.SemaphoreType.DMA((2,))],
        compiler_params=params(WIDE),
        name="step",
    )(info, own, other, high, low)


def last(scale, info, own, other, high, low):
    length, rank, rows = own.shape
    held, both = scratch(length, rank, high.shape[0])
    shapes = [(2, 5 * rank // 4, LANES), (rank, rows)]
    return pl.pallas_call(
        functools.partial(last_kernel, scale),
        in_specs=[SMEM_SPEC, VMEM_SPEC, VMEM_SPEC, HBM_SPEC, HBM_SPEC],
        out_shape=[jax.ShapeDtypeStruct(x, F32) for x in shapes],
        scratch_shapes=held + both + [pltpu.SemaphoreType.DMA((2,))],
        compiler_params=params(WIDE),
        name="last",
    )(info, own, other, high, low)


def columns_of(top, low):
    half = top.shape[0] * 2 // 5
    quarter = half // 2
    lane = lax.broadcasted_iota(jnp.int32, (quarter, LANES), 1)
    blocks = []
    for x in (top, low):
        tail = x[2 * half :]
        upper = jnp.where(lane < LANES // 2, tail, 0.0)
        lower = jnp.where(lane < LANES // 2, pltpu.roll(tail, LANES // 2, 1), 0.0)
        blocks.append((x[:half], x[half : 2 * half], jnp.concatenate([upper, lower], axis=0)))
    return [jnp.concatenate([a, b], axis=0) for a, b in zip(*blocks)]


def finish_kernel(flag, grads, errors, own, other, basis, new_errors, factor_q):
    first_core = flag[0] == 0
    turned = basis[...].T
    b_high, b_low = split2(turned)
    left = jnp.concatenate([b_high, b_high, b_low], axis=1)
    wide = 5 * LANES
    lane = lax.broadcasted_iota(jnp.int32, (basis.shape[0], LANES), 1)
    for i in range(own.shape[0] // 2):
        even, odd = [
            columns_of(jnp.where(first_core, own[j], other[j]), jnp.where(first_core, other[j], own[j]))
            for j in (2 * i, 2 * i + 1)
        ]
        turn = [pltpu.roll(x, LANES // 2, 1) for x in odd]
        low_lane = lane < LANES // 2
        q = jnp.concatenate(
            [
                even[0],
                even[1],
                jnp.where(low_lane, even[2], turn[0]),
                jnp.where(low_lane, turn[0], turn[1]),
                jnp.where(low_lane, turn[1], turn[2]),
            ],
            axis=1,
        )
        span = slice(i * wide, (i + 1) * wide)
        factor_q[:, span] = q
        q_high, q_low = split2(q)
        product = dot(left, jnp.concatenate([q_high, q_low, q_high], axis=0), NN)
        merged = grads[:, span].astype(F32) + errors[:, span].astype(F32)
        new_errors[:, span] = (merged - product).astype(BF16)


def finish(flag, grads, errors, own, other, basis):
    rows, width = grads.shape
    reps, tall, lanes = own.shape
    rank = basis.shape[0]
    steps = 4
    cols = pl.BlockSpec((rows, width // steps), lambda i: (0, i))
    piece = pl.BlockSpec((reps // steps, tall, lanes), lambda i: (i, 0, 0))
    return pl.pallas_call(
        finish_kernel,
        grid=(steps,),
        in_specs=[SMEM_SPEC, cols, cols, piece, piece, pl.BlockSpec((rank, rows), lambda i: (0, 0))],
        out_specs=[cols, pl.BlockSpec((rank, width // steps), lambda i: (0, i))],
        out_shape=[jax.ShapeDtypeStruct((rows, width), BF16), jax.ShapeDtypeStruct((rank, width), F32)],
        compiler_params=params(),
        name="finish",
    )(flag, grads, errors, own, other, basis)


def exchange(chunks, axis):
    return lax.all_to_all(chunks, axis, 0, 0)


def gather(block, axis, count):
    return exchange(jnp.broadcast_to(block[None], (count,) + block.shape), axis)


def swap_cores(block):
    return lax.ppermute(block, "core", [(0, 1), (1, 0)])


def ring(block, length):
    half = length // 2
    blocks = [block]
    for s in range(1, half, 2):
        for far in (2, 1):
            up = [(2 * i, 2 * ((i + far) % length)) for i in range(length)]
            down = [(2 * i + 1, 2 * ((i - far) % length) + 1) for i in range(length)]
            pairs = up + down if s + far - 1 < half else down
            blocks.insert(s, lax.ppermute(blocks[s - 1], ("z", "core"), pairs))
    return blocks


def body(grads, errors, q_start):
    grads, errors = grads[0], errors[0]
    rows, width = grads.shape
    rank = q_start.shape[0]
    reps, length = lax.axis_size("rep"), lax.axis_size("z")
    core, place = lax.axis_index("core"), lax.axis_index("z")
    cut, extra = width // reps, rank // reps
    scale = 1.0 / reps
    flag = core.reshape(1).astype(jnp.int32)
    info = jnp.stack([place, core]).astype(jnp.int32)

    block = jnp.sum(exchange(start(grads, errors, q_start, reps), "rep"), axis=0)
    streams = ring(block, length), ring(swap_cores(block), length)
    held = jnp.stack(
        [jnp.stack([jnp.where(core == 0, x[j], x[j + 1]) for x in streams]) for j in range(length // 2)]
    )
    total = held[:, :, :cut]
    piece = held[:, :, cut : cut + extra]
    piece = jnp.where(core == 0, piece, piece[:, ::-1]).reshape(length * extra, rows)
    own = gather(piece, "rep", reps).reshape(reps, length, extra, rows)
    own = own.transpose(1, 0, 2, 3).reshape(length, rank, rows)
    partial, high, low = first(scale, info, own, swap_cores(own), total, swap_cores(total))
    for turn in range(ITERS - 1):
        own = gather(jnp.sum(exchange(partial, "rep"), axis=0), "rep", reps)
        if turn < ITERS - 2:
            partial = step(scale, info, own, swap_cores(own), high, low)
    part_q, basis = last(scale, info, own, swap_cores(own), high, low)
    own_q = gather(lax.dynamic_index_in_dim(part_q, core, 0, False), "rep", reps)
    new_errors, factor_q = finish(flag, grads, errors, own_q, swap_cores(own_q), basis)
    return new_errors[None], factor_q


def solution(mesh):
    reps, count = mesh.devices.shape
    split = Mesh(mesh.devices.reshape(reps, count // 2, 2), ("rep", "z", "core"))
    placed = P("rep", ("z", "core"), None)
    return jax.shard_map(
        body, mesh=split, in_specs=(placed, placed, P()), out_specs=(placed, P()), check_vma=False
    )
```

```python
import functools

import jax
import jax.numpy as jnp
from jax import lax
from jax.experimental import pallas as pl
from jax.experimental.pallas import tpu as pltpu
from jax.sharding import Mesh, PartitionSpec as P

ITERS = 3
F32 = jnp.float32
BF16 = jnp.bfloat16
LANES = 128
VMEM = 20 * 1024 * 1024
SMEM_SPEC = pl.BlockSpec(memory_space=pltpu.SMEM)
VMEM_SPEC = pl.BlockSpec(memory_space=pltpu.VMEM)
HBM_SPEC = pl.BlockSpec(memory_space=pltpu.HBM)
NT = (((1,), (1,)), ((), ()))
NN = (((1,), (0,)), ((), ()))


def dot(a, b, dims):
    return lax.dot_general(a, b, dims, preferred_element_type=F32)


def split2(x):
    high = x.astype(BF16)
    return high, (x - high.astype(F32)).astype(BF16)


def split3(x):
    high = x.astype(BF16)
    rest = x - high.astype(F32)
    mid = rest.astype(BF16)
    return high, mid, (rest - mid.astype(F32)).astype(BF16)


def params(limit=VMEM):
    return pltpu.CompilerParams(vmem_limit_bytes=limit)


def start_kernel(grads, errors, q_start, out, g_held, e_held, q_held, sems):
    reps, tall, rows = out.shape
    rank, width = q_start.shape
    cut = width // reps
    extra = rank // reps
    spans = [pl.ds(2 * cut * i, 2 * cut) for i in range(reps // 2)]
    loads = []
    for i, span in enumerate(spans):
        pairs = ((grads, g_held), (errors, e_held), (q_start, q_held))
        loads.append(
            [pltpu.make_async_copy(x.at[:, span], y.at[:, span], sems.at[k, i]) for k, (x, y) in enumerate(pairs)]
        )
        for load in loads[-1]:
            load.start()
    left = jnp.zeros((2 * rank, rows), F32)
    for i, span in enumerate(spans):
        for load in loads[i]:
            load.wait()
        g, e = g_held[:, span], e_held[:, span]
        turned = (g.astype(F32) + e.astype(F32)).T
        out[2 * i, :cut, :] = turned[:cut]
        out[2 * i + 1, :cut, :] = turned[cut:]
        high, low = split2(q_held[:, span])
        both = jnp.concatenate([high, low], axis=0)
        left = left + (dot(both, g, NT) + dot(both, e, NT))
    left = left[:rank] + left[rank:]
    for i in range(reps):
        out[i, cut : cut + extra, :] = left[extra * i : extra * (i + 1)]
        out[i, cut + extra :, :] = jnp.zeros((tall - cut - extra, rows), F32)


def start(grads, errors, q_start, reps):
    rows, width = grads.shape
    tall = width // reps + 8
    return pl.pallas_call(
        start_kernel,
        in_specs=[HBM_SPEC] * 3,
        out_specs=VMEM_SPEC,
        out_shape=jax.ShapeDtypeStruct((reps, tall, rows), F32),
        scratch_shapes=[
            pltpu.VMEM(grads.shape, BF16),
            pltpu.VMEM(errors.shape, BF16),
            pltpu.VMEM(q_start.shape, F32),
            pltpu.SemaphoreType.DMA((3, reps // 2)),
        ],
        compiler_params=params(3 * VMEM),
        name="start",
    )(grads, errors, q_start)


def inverse_factor(gram_twice):
    rank, wide = gram_twice.shape
    step = 8
    count = rank // step
    row = lax.broadcasted_iota(jnp.int32, (step, wide), 0)
    col = lax.broadcasted_iota(jnp.int32, (step, wide), 1)
    a = []
    for b in range(count):
        unit = (col == row + (rank + b * step)).astype(F32)
        a.append(jnp.where(col < rank, gram_twice[b * step : (b + 1) * step], unit))

    def spread(x, k):
        return jnp.broadcast_to(x[:, k : k + 1], (step, wide))

    def line_of(x, j):
        return jnp.broadcast_to(x[j : j + 1, :], (step, wide))

    done = []
    for p in range(count):
        panel = a[p]
        f = [spread(panel, p * step + j) for j in range(step)]
        pivots = jnp.ones((step, wide), F32)
        lines, weight = [], []
        for j in range(step):
            pivot = line_of(f[j], j)
            inverse = 1.0 / pivot
            below = jnp.where(row > j, f[j], 0.0)
            line = line_of(panel, j) * inverse
            panel = panel - below * line
            ahead = {}
            for t in range(j + 1, step):
                ahead[t] = line_of(f[t], j) * inverse
                f[t] = f[t] - below * ahead[t]
            pivots = jnp.where(row == j, pivot, pivots)
            lines.append(line)
            weight.append(ahead)
        done.append(jnp.where(col < rank, 0.0, panel * lax.rsqrt(pivots)))
        for b in range(p + 1, count):
            g = [spread(a[b], p * step + j) for j in range(step)]
            for j in range(step):
                for t in range(j + 1, step):
                    g[t] = g[t] - g[j] * weight[j][t]
                a[b] = a[b] - g[j] * lines[j]
    w = jnp.concatenate(done, axis=0)
    return w + pltpu.roll(w, rank, 1)


def gram_of(held, chunk):
    rank = held.shape[0] // 4
    total = jnp.zeros((3 * rank, 4 * rank), F32)
    for at in range(0, held.shape[1], chunk):
        x = held[:, at : at + chunk]
        total = total + dot(x[: 3 * rank], x, NT)
    total = total[:rank] + (total[rank : 2 * rank] + total[2 * rank :])
    near, far = total[:, : 2 * rank], total[:, 2 * rank :]
    return near + pltpu.roll(near, rank, 1) + far


def put(held, at, x):
    rank, n = x.shape
    high, mid, low = split3(x)
    span = pl.ds(at, n)
    held[:rank, span] = high
    held[rank : 2 * rank, span] = mid
    held[2 * rank : 3 * rank, span] = low
    held[3 * rank :, span] = low


def weights(w):
    rank = w.shape[0]
    col = lax.broadcasted_iota(jnp.int32, w.shape, 1)
    once = jnp.where(col < rank, w, 0.0)
    wide = jnp.concatenate([w, once], axis=1)
    return jnp.concatenate(split3(wide), axis=0)


CHUNK = 512


def right_of(held, high, low):
    rank = held.shape[0] // 4
    cut, n = high.shape
    one = jnp.zeros((2 * rank, cut), F32)
    two = jnp.zeros((rank, cut), F32)
    for at in range(0, n, CHUNK):
        x = held[: 2 * rank, at : at + CHUNK]
        one = one + dot(x, high[:, at : at + CHUNK], NT)
        two = two + dot(x[:rank], low[:, at : at + CHUNK], NT)
    return one[:rank] + (one[rank:] + two)


def planes(info, length, mine):
    upward = info[1] == (0 if mine else 1)
    columns = 2 * LANES

    def at(j):
        plane = lax.rem(info[0] + jnp.where(upward, length - j, 1 + j), length)
        return pl.multiple_of(plane * columns, columns)

    return at


def whiten(held):
    rank = held.shape[0] // 4
    left = weights(inverse_factor(gram_of(held, CHUNK)))
    for at in range(0, held.shape[1], CHUNK):
        y = dot(left, held[:, at : at + CHUNK], NN)
        put(held, at, y[:rank] + (y[rank : 2 * rank] + y[2 * rank :]))
    return inverse_factor(gram_of(held, CHUNK))


def orthonormal(info, own, other, held):
    length = own.shape[0]
    for mine, blocks in ((True, own), (False, other)):
        at = planes(info, length, mine)
        for j in range(length // 2):
            put(held, at(j), jnp.concatenate([blocks[2 * j], blocks[2 * j + 1]], axis=1))
    return whiten(held)


def right_factor(scale, second, held, high, low):
    left = second[:, : second.shape[0]] * scale
    right = right_of(held, high, low)
    return jnp.dot(left, right, precision=lax.Precision.HIGHEST, preferred_element_type=F32)


def next_left(info, q, high, low, out):
    length, rank, rows = out.shape
    q_high, q_low = split2(q)
    both = jnp.concatenate([q_high, q_low], axis=0)
    at = planes(info, length, True)
    for j in range(length // 2):
        span = pl.ds(at(j), 2 * rows)
        one = dot(both, high[:, span], NN)
        x = one[:rank] + (one[rank:] + dot(q_high, low[:, span], NN))
        out[2 * j] = x[:, :rows]
        out[2 * j + 1] = x[:, rows:]


def orth_kernel(info, own, other, rows_out, weights_out, held):
    weights_out[...] = orthonormal(info, own, other, held)
    rows_out[...] = held[...]


def first_kernel(scale, info, held, second, total, total_other, out, high_out, low_out, high, low, sems):
    length = out.shape[0]
    for mine, blocks in ((True, total), (False, total_other)):
        at = planes(info, length, mine)
        core = info[1] if mine else 1 - info[1]
        for j in range(length // 2):
            for stream in range(2):
                side = core if stream == 0 else 1 - core
                span = pl.ds(pl.multiple_of(at(j) + side * LANES, LANES), LANES)
                high[:, span], low[:, span] = split2(blocks[j, stream])
    stores = [
        pltpu.make_async_copy(high, high_out, sems.at[0]),
        pltpu.make_async_copy(low, low_out, sems.at[1]),
    ]
    for store in stores:
        store.start()
    next_left(info, right_factor(scale, second[...], held, high, low), high, low, out)
    for store in stores:
        store.wait()


def load_parts(high_in, low_in, high, low, sems):
    loads = [
        pltpu.make_async_copy(high_in, high, sems.at[0]),
        pltpu.make_async_copy(low_in, low, sems.at[1]),
    ]
    for load in loads:
        load.start()
    return loads


def step_kernel(scale, info, own, other, high_in, low_in, out, held, high, low, sems):
    loads = load_parts(high_in, low_in, high, low, sems)
    second = orthonormal(info, own, other, held)
    for load in loads:
        load.wait()
    next_left(info, right_factor(scale, second, held, high, low), high, low, out)


def last_kernel(scale, info, own, other, high_in, low_in, out, basis, held, high, low, sems):
    loads = load_parts(high_in, low_in, high, low, sems)
    length, rank, rows = own.shape
    second = orthonormal(info, own, other, held)
    for load in loads:
        load.wait()
    q = right_factor(scale, second, held, high, low)
    half = rank // 2
    quarter = half // 2
    rest = jnp.concatenate([q[:, 2 * LANES :], jnp.zeros_like(q[:, 2 * LANES :])], axis=1)
    for core in range(2):
        span = slice(core * half, (core + 1) * half)
        out[core, :half] = q[span, :LANES]
        out[core, half : 2 * half] = q[span, LANES : 2 * LANES]
        tail = rest[span]
        out[core, 2 * half :] = tail[:quarter] + pltpu.roll(tail[quarter:], LANES // 2, 1)
    at = pl.multiple_of((2 * info[0] + info[1]) * rows, rows)
    y = dot(weights(second), held[:, pl.ds(at, rows)], NN)
    basis[...] = y[:rank] + (y[rank : 2 * rank] + y[2 * rank :])


def scratch(length, rank, cut):
    n = 2 * length * LANES
    return [pltpu.VMEM((4 * rank, n), BF16)], [pltpu.VMEM((cut, n), BF16)] * 2


def orth(info, own, other):
    length, rank, rows = own.shape
    shape = (4 * rank, 2 * length * rows)
    return pl.pallas_call(
        orth_kernel,
        in_specs=[SMEM_SPEC, VMEM_SPEC, VMEM_SPEC],
        out_shape=[jax.ShapeDtypeStruct(shape, BF16), jax.ShapeDtypeStruct((rank, 2 * rank), F32)],
        scratch_shapes=[pltpu.VMEM(shape, BF16)],
        compiler_params=params(),
        name="orth",
    )(info, own, other)


def first(scale, info, held, second, total, total_other, shape):
    length, rank, rows = shape
    cut = total.shape[2]
    _, both = scratch(length, rank, cut)
    whole = jax.ShapeDtypeStruct((cut, 2 * length * rows), BF16)
    return pl.pallas_call(
        functools.partial(first_kernel, scale),
        in_specs=[SMEM_SPEC] + [VMEM_SPEC] * 4,
        out_specs=[VMEM_SPEC, HBM_SPEC, HBM_SPEC],
        out_shape=[jax.ShapeDtypeStruct(shape, F32), whole, whole],
        scratch_shapes=both + [pltpu.SemaphoreType.DMA((2,))],
        compiler_params=params(),
        name="first",
    )(info, held, second, total, total_other)


def step(scale, info, own, other, high, low):
    length, rank, rows = own.shape
    held, both = scratch(length, rank, high.shape[0])
    return pl.pallas_call(
        functools.partial(step_kernel, scale),
        in_specs=[SMEM_SPEC, VMEM_SPEC, VMEM_SPEC, HBM_SPEC, HBM_SPEC],
        out_shape=jax.ShapeDtypeStruct(own.shape, F32),
        scratch_shapes=held + both + [pltpu.SemaphoreType.DMA((2,))],
        compiler_params=params(),
        name="step",
    )(info, own, other, high, low)


def last(scale, info, own, other, high, low):
    length, rank, rows = own.shape
    held, both = scratch(length, rank, high.shape[0])
    shapes = [(2, 5 * rank // 4, LANES), (rank, rows)]
    return pl.pallas_call(
        functools.partial(last_kernel, scale),
        in_specs=[SMEM_SPEC, VMEM_SPEC, VMEM_SPEC, HBM_SPEC, HBM_SPEC],
        out_shape=[jax.ShapeDtypeStruct(x, F32) for x in shapes],
        scratch_shapes=held + both + [pltpu.SemaphoreType.DMA((2,))],
        compiler_params=params(),
        name="last",
    )(info, own, other, high, low)


def columns_of(top, low):
    half = top.shape[0] * 2 // 5
    quarter = half // 2
    lane = lax.broadcasted_iota(jnp.int32, (quarter, LANES), 1)
    blocks = []
    for x in (top, low):
        tail = x[2 * half :]
        upper = jnp.where(lane < LANES // 2, tail, 0.0)
        lower = jnp.where(lane < LANES // 2, pltpu.roll(tail, LANES // 2, 1), 0.0)
        blocks.append((x[:half], x[half : 2 * half], jnp.concatenate([upper, lower], axis=0)))
    return [jnp.concatenate([a, b], axis=0) for a, b in zip(*blocks)]


def finish_kernel(flag, grads, errors, own, other, basis, new_errors, factor_q):
    first_core = flag[0] == 0
    turned = basis[...].T
    b_high, b_low = split2(turned)
    left = jnp.concatenate([b_high, b_high, b_low], axis=1)
    wide = 5 * LANES
    lane = lax.broadcasted_iota(jnp.int32, (basis.shape[0], LANES), 1)
    for i in range(own.shape[0] // 2):
        even, odd = [
            columns_of(jnp.where(first_core, own[j], other[j]), jnp.where(first_core, other[j], own[j]))
            for j in (2 * i, 2 * i + 1)
        ]
        turn = [pltpu.roll(x, LANES // 2, 1) for x in odd]
        low_lane = lane < LANES // 2
        q = jnp.concatenate(
            [
                even[0],
                even[1],
                jnp.where(low_lane, even[2], turn[0]),
                jnp.where(low_lane, turn[0], turn[1]),
                jnp.where(low_lane, turn[1], turn[2]),
            ],
            axis=1,
        )
        span = slice(i * wide, (i + 1) * wide)
        factor_q[:, span] = q
        q_high, q_low = split2(q)
        product = dot(left, jnp.concatenate([q_high, q_low, q_high], axis=0), NN)
        merged = grads[:, span].astype(F32) + errors[:, span].astype(F32)
        new_errors[:, span] = (merged - product).astype(BF16)


def finish(flag, grads, errors, own, other, basis):
    rows, width = grads.shape
    reps, tall, lanes = own.shape
    rank = basis.shape[0]
    steps = 4
    cols = pl.BlockSpec((rows, width // steps), lambda i: (0, i))
    piece = pl.BlockSpec((reps // steps, tall, lanes), lambda i: (i, 0, 0))
    return pl.pallas_call(
        finish_kernel,
        grid=(steps,),
        in_specs=[SMEM_SPEC, cols, cols, piece, piece, pl.BlockSpec((rank, rows), lambda i: (0, 0))],
        out_specs=[cols, pl.BlockSpec((rank, width // steps), lambda i: (0, i))],
        out_shape=[jax.ShapeDtypeStruct((rows, width), BF16), jax.ShapeDtypeStruct((rank, width), F32)],
        compiler_params=params(),
        name="finish",
    )(flag, grads, errors, own, other, basis)


def exchange(chunks, axis):
    return lax.all_to_all(chunks, axis, 0, 0)


def gather(block, axis, count):
    return exchange(jnp.broadcast_to(block[None], (count,) + block.shape), axis)


def swap_cores(block):
    return lax.ppermute(block, "core", [(0, 1), (1, 0)])


def along_ring(block, length, far, both=True):
    up = [(2 * i, 2 * ((i + far) % length)) for i in range(length)]
    down = [(2 * i + 1, 2 * ((i - far) % length) + 1) for i in range(length)]
    return lax.ppermute(block, ("z", "core"), up + down if both else down)


def after(x, earlier):
    return lax.optimization_barrier((x, earlier))[0]


def body(grads, errors, q_start):
    grads, errors = grads[0], errors[0]
    rows, width = grads.shape
    rank = q_start.shape[0]
    reps, length = lax.axis_size("rep"), lax.axis_size("z")
    core, place = lax.axis_index("core"), lax.axis_index("z")
    cut, extra = width // reps, rank // reps
    half = length // 2
    scale = 1.0 / reps
    flag = core.reshape(1).astype(jnp.int32)
    info = jnp.stack([place, core]).astype(jnp.int32)

    block = jnp.sum(exchange(start(grads, errors, q_start, reps), "rep"), axis=0)
    other = swap_cores(block)
    now = [block[:cut], other[:cut]]
    pieces = jnp.stack([block[cut : cut + extra], other[cut : cut + extra]])[None]
    pieces = jnp.where(core == 0, pieces, pieces[:, ::-1])
    held = []
    reach = 1
    for s in range(half):
        later = [along_ring(x, length, 1, s < half - 1) for x in now]
        held.append([now, later])
        if reach < half:
            pieces = jnp.concatenate([pieces, along_ring(pieces, length, reach)], axis=0)
            reach *= 2
            later[0] = after(later[0], pieces)
        elif reach == half:
            shifted = along_ring(pieces, length, 1, False)
            pieces = jnp.where(core == 0, pieces, shifted).reshape(length * extra, rows)
            reach *= 2
            later[0] = after(later[0], pieces)
            own = gather(pieces, "rep", reps).reshape(reps, length, extra, rows)
            own = own.transpose(1, 0, 2, 3).reshape(length, rank, rows)
        elif s == half - 2:
            later[0] = after(later[0], own)
        now = later
    total = jnp.stack([jnp.stack([jnp.where(core == 0, x, y) for x, y in zip(*pair)]) for pair in held])
    rows_of, weight = orth(info, own, swap_cores(own))
    partial, high, low = first(scale, info, rows_of, weight, total, swap_cores(total), own.shape)
    for turn in range(ITERS - 1):
        own = gather(jnp.sum(exchange(partial, "rep"), axis=0), "rep", reps)
        if turn < ITERS - 2:
            partial = step(scale, info, own, swap_cores(own), high, low)
    part_q, basis = last(scale, info, own, swap_cores(own), high, low)
    own_q = gather(lax.dynamic_index_in_dim(part_q, core, 0, False), "rep", reps)
    new_errors, factor_q = finish(flag, grads, errors, own_q, swap_cores(own_q), basis)
    return new_errors[None], factor_q


def solution(mesh):
    reps, count = mesh.devices.shape
    split = Mesh(mesh.devices.reshape(reps, count // 2, 2), ("rep", "z", "core"))
    placed = P("rep", ("z", "core"), None)
    return jax.shard_map(
        body, mesh=split, in_specs=(placed, placed, P()), out_specs=(placed, P()), check_vma=False
    )
```

```python
import functools

import jax
import jax.numpy as jnp
from jax import lax
from jax.experimental import pallas as pl
from jax.experimental.pallas import tpu as pltpu
from jax.sharding import Mesh, PartitionSpec as P

ITERS = 3
F32 = jnp.float32
BF16 = jnp.bfloat16
LANES = 128
VMEM = 20 * 1024 * 1024
SMEM_SPEC = pl.BlockSpec(memory_space=pltpu.SMEM)
VMEM_SPEC = pl.BlockSpec(memory_space=pltpu.VMEM)
HBM_SPEC = pl.BlockSpec(memory_space=pltpu.HBM)
NT = (((1,), (1,)), ((), ()))
NN = (((1,), (0,)), ((), ()))


def dot(a, b, dims):
    return lax.dot_general(a, b, dims, preferred_element_type=F32)


def split2(x):
    high = x.astype(BF16)
    return high, (x - high.astype(F32)).astype(BF16)


def split3(x):
    high = x.astype(BF16)
    rest = x - high.astype(F32)
    mid = rest.astype(BF16)
    return high, mid, (rest - mid.astype(F32)).astype(BF16)


def params(limit=VMEM):
    return pltpu.CompilerParams(vmem_limit_bytes=limit)


def start_kernel(grads, errors, q_start, out, g_held, e_held, q_held, sems):
    reps, tall, rows = out.shape
    rank, width = q_start.shape
    cut = width // reps
    extra = rank // reps
    spans = [pl.ds(2 * cut * i, 2 * cut) for i in range(reps // 2)]
    loads = []
    for i, span in enumerate(spans):
        pairs = ((grads, g_held), (errors, e_held), (q_start, q_held))
        loads.append(
            [pltpu.make_async_copy(x.at[:, span], y.at[:, span], sems.at[k, i]) for k, (x, y) in enumerate(pairs)]
        )
        for load in loads[-1]:
            load.start()
    left = jnp.zeros((2 * rank, rows), F32)
    for i, span in enumerate(spans):
        for load in loads[i]:
            load.wait()
        g, e = g_held[:, span], e_held[:, span]
        turned = (g.astype(F32) + e.astype(F32)).T
        out[2 * i, :cut, :] = turned[:cut]
        out[2 * i + 1, :cut, :] = turned[cut:]
        high, low = split2(q_held[:, span])
        both = jnp.concatenate([high, low], axis=0)
        left = left + (dot(both, g, NT) + dot(both, e, NT))
    left = left[:rank] + left[rank:]
    for i in range(reps):
        out[i, cut : cut + extra, :] = left[extra * i : extra * (i + 1)]
        out[i, cut + extra :, :] = jnp.zeros((tall - cut - extra, rows), F32)


def start(grads, errors, q_start, reps):
    rows, width = grads.shape
    tall = width // reps + 8
    return pl.pallas_call(
        start_kernel,
        in_specs=[HBM_SPEC] * 3,
        out_specs=VMEM_SPEC,
        out_shape=jax.ShapeDtypeStruct((reps, tall, rows), F32),
        scratch_shapes=[
            pltpu.VMEM(grads.shape, BF16),
            pltpu.VMEM(errors.shape, BF16),
            pltpu.VMEM(q_start.shape, F32),
            pltpu.SemaphoreType.DMA((3, reps // 2)),
        ],
        compiler_params=params(3 * VMEM),
        name="start",
    )(grads, errors, q_start)


def inverse_factor(gram_twice):
    rank, wide = gram_twice.shape
    step = 8
    count = rank // step
    row = lax.broadcasted_iota(jnp.int32, (step, wide), 0)
    col = lax.broadcasted_iota(jnp.int32, (step, wide), 1)

    def spread(x, k):
        return jnp.broadcast_to(x[:, k : k + 1], (step, wide))

    def line_of(x, j):
        return jnp.broadcast_to(x[j : j + 1, :], (step, wide))

    parts = [gram_twice[b * step : (b + 1) * step] for b in range(count)]
    near = [jnp.where(col == row + b * step, parts[b], 0.0) for b in range(count)]
    both = sum(jnp.where(col == row + (rank + b * step), parts[b], near[b]) for b in range(count))
    across = lax.rsqrt(jnp.sum(both, axis=0, keepdims=True))
    a = []
    for b in range(count):
        down = lax.rsqrt(jnp.sum(near[b], axis=1, keepdims=True))
        unit = (col == row + (rank + b * step)).astype(F32)
        a.append(jnp.where(col < rank, parts[b] * down * across, unit))

    done = []
    for p in range(count):
        panel = a[p]
        f = [spread(panel, p * step + j) for j in range(step)]
        pivots = jnp.ones((step, wide), F32)
        pairs = []
        for j in range(0, step, 2):
            x, z, y = line_of(f[j], j), line_of(f[j], j + 1), line_of(f[j + 1], j + 1)
            det = x * y - z * z
            inverse = 1.0 / det

            def solve(v):
                top, low = line_of(v, j), line_of(v, j + 1)
                return (y * top - z * low) * inverse, (x * low - z * top) * inverse

            below = [jnp.where(row > j + 1, f[j + i], 0.0) for i in range(2)]
            ahead = {}
            for t in range(j + 2, step):
                ahead[t] = solve(f[t])
                f[t] = f[t] - (below[0] * ahead[t][0] + below[1] * ahead[t][1])
            line = solve(panel)
            ratio = 1.0 / x
            second = line_of(panel, j + 1) - (z * ratio) * line_of(panel, j)
            panel = panel - (below[0] * line[0] + below[1] * line[1])
            panel = jnp.where(row == j + 1, second, panel)
            pivots = jnp.where(row == j, x, jnp.where(row == j + 1, det * ratio, pivots))
            pairs.append((line, ahead))
        done.append(jnp.where(col < rank, 0.0, panel * lax.rsqrt(pivots) * across))
        for b in range(p + 1, count):
            g = [spread(a[b], p * step + j) for j in range(step)]
            for j, (line, ahead) in zip(range(0, step, 2), pairs):
                for t in range(j + 2, step):
                    g[t] = g[t] - (g[j] * ahead[t][0] + g[j + 1] * ahead[t][1])
                a[b] = a[b] - (g[j] * line[0] + g[j + 1] * line[1])
    w = jnp.concatenate(done, axis=0)
    return w + pltpu.roll(w, rank, 1)


def gram_of(held, chunk):
    rank = held.shape[0] // 4
    total = jnp.zeros((3 * rank, 4 * rank), F32)
    for at in range(0, held.shape[1], chunk):
        x = held[:, at : at + chunk]
        total = total + dot(x[: 3 * rank], x, NT)
    total = total[:rank] + (total[rank : 2 * rank] + total[2 * rank :])
    near, far = total[:, : 2 * rank], total[:, 2 * rank :]
    return near + pltpu.roll(near, rank, 1) + far


def put(held, at, x):
    rank, n = x.shape
    high, mid, low = split3(x)
    span = pl.ds(at, n)
    held[:rank, span] = high
    held[rank : 2 * rank, span] = mid
    held[2 * rank : 3 * rank, span] = low
    held[3 * rank :, span] = low


def weights(w):
    rank = w.shape[0]
    col = lax.broadcasted_iota(jnp.int32, w.shape, 1)
    once = jnp.where(col < rank, w, 0.0)
    wide = jnp.concatenate([w, once], axis=1)
    return jnp.concatenate(split3(wide), axis=0)


CHUNK = 512


def right_of(held, high, low):
    rank = held.shape[0] // 4
    cut, n = high.shape
    one = jnp.zeros((2 * rank, cut), F32)
    two = jnp.zeros((rank, cut), F32)
    for at in range(0, n, CHUNK):
        x = held[: 2 * rank, at : at + CHUNK]
        one = one + dot(x, high[:, at : at + CHUNK], NT)
        two = two + dot(x[:rank], low[:, at : at + CHUNK], NT)
    return one[:rank] + (one[rank:] + two)


def planes(info, length, mine):
    upward = info[1] == (0 if mine else 1)
    columns = 2 * LANES

    def at(j):
        plane = lax.rem(info[0] + jnp.where(upward, length - j, 1 + j), length)
        return pl.multiple_of(plane * columns, columns)

    return at


def orthonormal(info, own, other, held):
    length = own.shape[0]
    for mine, blocks in ((True, own), (False, other)):
        at = planes(info, length, mine)
        for j in range(length // 2):
            put(held, at(j), jnp.concatenate([blocks[2 * j], blocks[2 * j + 1]], axis=1))
    left = weights(inverse_factor(gram_of(held, CHUNK)))
    for at in range(0, held.shape[1], CHUNK):
        y = dot(left, held[:, at : at + CHUNK], NN)
        put(held, at, y[: y.shape[0] // 3] + (y[y.shape[0] // 3 : 2 * y.shape[0] // 3] + y[2 * y.shape[0] // 3 :]))
    return inverse_factor(gram_of(held, CHUNK))


def right_factor(scale, second, held, high, low):
    left = second[:, : second.shape[0]] * scale
    right = right_of(held, high, low)
    return jnp.dot(left, right, precision=lax.Precision.HIGHEST, preferred_element_type=F32)


def next_left(info, q, high, low, out):
    length, rank, rows = out.shape
    q_high, q_low = split2(q)
    both = jnp.concatenate([q_high, q_low], axis=0)
    at = planes(info, length, True)
    for j in range(length // 2):
        span = pl.ds(at(j), 2 * rows)
        one = dot(both, high[:, span], NN)
        x = one[:rank] + (one[rank:] + dot(q_high, low[:, span], NN))
        out[2 * j] = x[:, :rows]
        out[2 * j + 1] = x[:, rows:]


def parts_kernel(info, total, total_other, high, low):
    half = total.shape[0]
    for mine, blocks in ((True, total), (False, total_other)):
        at = planes(info, 2 * half, mine)
        core = info[1] if mine else 1 - info[1]
        for j in range(half):
            for stream in range(2):
                side = core if stream == 0 else 1 - core
                span = pl.ds(pl.multiple_of(at(j) + side * LANES, LANES), LANES)
                high[:, span], low[:, span] = split2(blocks[j, stream])


def load_parts(high_in, low_in, high, low, sems):
    loads = [
        pltpu.make_async_copy(high_in, high, sems.at[0]),
        pltpu.make_async_copy(low_in, low, sems.at[1]),
    ]
    for load in loads:
        load.start()
    return loads


def step_kernel(scale, info, own, other, high_in, low_in, out, held, high, low, sems):
    loads = load_parts(high_in, low_in, high, low, sems)
    second = orthonormal(info, own, other, held)
    for load in loads:
        load.wait()
    next_left(info, right_factor(scale, second, held, high, low), high, low, out)


def last_kernel(scale, info, own, other, high_in, low_in, out, basis, held, high, low, sems):
    loads = load_parts(high_in, low_in, high, low, sems)
    length, rank, rows = own.shape
    second = orthonormal(info, own, other, held)
    for load in loads:
        load.wait()
    q = right_factor(scale, second, held, high, low)
    half = rank // 2
    quarter = half // 2
    rest = jnp.concatenate([q[:, 2 * LANES :], jnp.zeros_like(q[:, 2 * LANES :])], axis=1)
    for core in range(2):
        span = slice(core * half, (core + 1) * half)
        out[core, :half] = q[span, :LANES]
        out[core, half : 2 * half] = q[span, LANES : 2 * LANES]
        tail = rest[span]
        out[core, 2 * half :] = tail[:quarter] + pltpu.roll(tail[quarter:], LANES // 2, 1)
    at = pl.multiple_of((2 * info[0] + info[1]) * rows, rows)
    y = dot(weights(second), held[:, pl.ds(at, rows)], NN)
    basis[...] = y[:rank] + (y[rank : 2 * rank] + y[2 * rank :])


def scratch(length, rank, cut):
    n = 2 * length * LANES
    return [pltpu.VMEM((4 * rank, n), BF16)], [pltpu.VMEM((cut, n), BF16)] * 2


def parts(info, total, total_other):
    half, cores, cut, rows = total.shape
    whole = jax.ShapeDtypeStruct((cut, 2 * half * cores * rows), BF16)
    return pl.pallas_call(
        parts_kernel,
        in_specs=[SMEM_SPEC, VMEM_SPEC, VMEM_SPEC],
        out_shape=[whole, whole],
        compiler_params=params(),
        name="parts",
    )(info, total, total_other)


def step(scale, info, own, other, high, low):
    length, rank, rows = own.shape
    held, both = scratch(length, rank, high.shape[0])
    return pl.pallas_call(
        functools.partial(step_kernel, scale),
        in_specs=[SMEM_SPEC, VMEM_SPEC, VMEM_SPEC, HBM_SPEC, HBM_SPEC],
        out_shape=jax.ShapeDtypeStruct(own.shape, F32),
        scratch_shapes=held + both + [pltpu.SemaphoreType.DMA((2,))],
        compiler_params=params(),
        name="step",
    )(info, own, other, high, low)


def last(scale, info, own, other, high, low):
    length, rank, rows = own.shape
    held, both = scratch(length, rank, high.shape[0])
    shapes = [(2, 5 * rank // 4, LANES), (rank, rows)]
    return pl.pallas_call(
        functools.partial(last_kernel, scale),
        in_specs=[SMEM_SPEC, VMEM_SPEC, VMEM_SPEC, HBM_SPEC, HBM_SPEC],
        out_shape=[jax.ShapeDtypeStruct(x, F32) for x in shapes],
        scratch_shapes=held + both + [pltpu.SemaphoreType.DMA((2,))],
        compiler_params=params(),
        name="last",
    )(info, own, other, high, low)


def columns_of(top, low):
    half = top.shape[0] * 2 // 5
    quarter = half // 2
    lane = lax.broadcasted_iota(jnp.int32, (quarter, LANES), 1)
    blocks = []
    for x in (top, low):
        tail = x[2 * half :]
        upper = jnp.where(lane < LANES // 2, tail, 0.0)
        lower = jnp.where(lane < LANES // 2, pltpu.roll(tail, LANES // 2, 1), 0.0)
        blocks.append((x[:half], x[half : 2 * half], jnp.concatenate([upper, lower], axis=0)))
    return [jnp.concatenate([a, b], axis=0) for a, b in zip(*blocks)]


def finish_kernel(flag, grads, errors, own, other, basis, new_errors, factor_q):
    first_core = flag[0] == 0
    turned = basis[...].T
    b_high, b_low = split2(turned)
    left = jnp.concatenate([b_high, b_high, b_low], axis=1)
    wide = 5 * LANES
    lane = lax.broadcasted_iota(jnp.int32, (basis.shape[0], LANES), 1)
    for i in range(own.shape[0] // 2):
        even, odd = [
            columns_of(jnp.where(first_core, own[j], other[j]), jnp.where(first_core, other[j], own[j]))
            for j in (2 * i, 2 * i + 1)
        ]
        turn = [pltpu.roll(x, LANES // 2, 1) for x in odd]
        low_lane = lane < LANES // 2
        q = jnp.concatenate(
            [
                even[0],
                even[1],
                jnp.where(low_lane, even[2], turn[0]),
                jnp.where(low_lane, turn[0], turn[1]),
                jnp.where(low_lane, turn[1], turn[2]),
            ],
            axis=1,
        )
        span = slice(i * wide, (i + 1) * wide)
        factor_q[:, span] = q
        q_high, q_low = split2(q)
        product = dot(left, jnp.concatenate([q_high, q_low, q_high], axis=0), NN)
        merged = grads[:, span].astype(F32) + errors[:, span].astype(F32)
        new_errors[:, span] = (merged - product).astype(BF16)


def finish(flag, grads, errors, own, other, basis):
    rows, width = grads.shape
    reps, tall, lanes = own.shape
    rank = basis.shape[0]
    steps = 4
    cols = pl.BlockSpec((rows, width // steps), lambda i: (0, i))
    piece = pl.BlockSpec((reps // steps, tall, lanes), lambda i: (i, 0, 0))
    return pl.pallas_call(
        finish_kernel,
        grid=(steps,),
        in_specs=[SMEM_SPEC, cols, cols, piece, piece, pl.BlockSpec((rank, rows), lambda i: (0, 0))],
        out_specs=[cols, pl.BlockSpec((rank, width // steps), lambda i: (0, i))],
        out_shape=[jax.ShapeDtypeStruct((rows, width), BF16), jax.ShapeDtypeStruct((rank, width), F32)],
        compiler_params=params(),
        name="finish",
    )(flag, grads, errors, own, other, basis)


def exchange(chunks, axis):
    return lax.all_to_all(chunks, axis, 0, 0)


def gather(block, axis, count):
    return exchange(jnp.broadcast_to(block[None], (count,) + block.shape), axis)


def swap_cores(block):
    return lax.ppermute(block, "core", [(0, 1), (1, 0)])


def ring(block, length):
    half = length // 2
    up = [(2 * i, 2 * ((i + 1) % length)) for i in range(length)]
    down = [(2 * i + 1, 2 * ((i - 1) % length) + 1) for i in range(length)]
    blocks = [block]
    for s in range(half):
        blocks.append(lax.ppermute(blocks[-1], ("z", "core"), up + down if s < half - 1 else down))
    return blocks


def body(grads, errors, q_start):
    grads, errors = grads[0], errors[0]
    rows, width = grads.shape
    rank = q_start.shape[0]
    reps, length = lax.axis_size("rep"), lax.axis_size("z")
    core, place = lax.axis_index("core"), lax.axis_index("z")
    cut, extra = width // reps, rank // reps
    scale = 1.0 / reps
    flag = core.reshape(1).astype(jnp.int32)
    info = jnp.stack([place, core]).astype(jnp.int32)

    block = jnp.sum(exchange(start(grads, errors, q_start, reps), "rep"), axis=0)
    streams = ring(block, length), ring(swap_cores(block), length)
    held = jnp.stack(
        [jnp.stack([jnp.where(core == 0, x[j], x[j + 1]) for x in streams]) for j in range(length // 2)]
    )
    total = held[:, :, :cut]
    piece = held[:, :, cut : cut + extra]
    piece = jnp.where(core == 0, piece, piece[:, ::-1]).reshape(length * extra, rows)
    own = gather(piece, "rep", reps).reshape(reps, length, extra, rows)
    own = own.transpose(1, 0, 2, 3).reshape(length, rank, rows)
    high, low = parts(info, total, swap_cores(total))
    for turn in range(ITERS - 1):
        partial = step(scale, info, own, swap_cores(own), high, low)
        own = gather(jnp.sum(exchange(partial, "rep"), axis=0), "rep", reps)
    part_q, basis = last(scale, info, own, swap_cores(own), high, low)
    own_q = gather(lax.dynamic_index_in_dim(part_q, core, 0, False), "rep", reps)
    new_errors, factor_q = finish(flag, grads, errors, own_q, swap_cores(own_q), basis)
    return new_errors[None], factor_q


def solution(mesh):
    reps, count = mesh.devices.shape
    split = Mesh(mesh.devices.reshape(reps, count // 2, 2), ("rep", "z", "core"))
    placed = P("rep", ("z", "core"), None)
    return jax.shard_map(
        body, mesh=split, in_specs=(placed, placed, P()), out_specs=(placed, P()), check_vma=False
    )
```

```python
import functools

import jax
import jax.numpy as jnp
from jax import lax
from jax.experimental import pallas as pl
from jax.experimental.pallas import tpu as pltpu
from jax.sharding import Mesh, PartitionSpec as P

ITERS = 3
F32 = jnp.float32
BF16 = jnp.bfloat16
LANES = 128
VMEM = 20 * 1024 * 1024
SMEM_SPEC = pl.BlockSpec(memory_space=pltpu.SMEM)
VMEM_SPEC = pl.BlockSpec(memory_space=pltpu.VMEM)
HBM_SPEC = pl.BlockSpec(memory_space=pltpu.HBM)
NT = (((1,), (1,)), ((), ()))
NN = (((1,), (0,)), ((), ()))


def dot(a, b, dims):
    return lax.dot_general(a, b, dims, preferred_element_type=F32)


def split2(x):
    high = x.astype(BF16)
    return high, (x - high.astype(F32)).astype(BF16)


def split3(x):
    high = x.astype(BF16)
    rest = x - high.astype(F32)
    mid = rest.astype(BF16)
    return high, mid, (rest - mid.astype(F32)).astype(BF16)


def params(limit=VMEM):
    return pltpu.CompilerParams(vmem_limit_bytes=limit)


def start_kernel(grads, errors, q_start, result, g_held, e_held, q_held, out, sems, out_sems):
    reps, tall, rows = out.shape
    rank, width = q_start.shape
    cut = width // reps
    extra = rank // reps
    spans = [pl.ds(2 * cut * i, 2 * cut) for i in range(reps // 2)]
    loads = []
    for i, span in enumerate(spans):
        pairs = ((grads, g_held), (errors, e_held), (q_start, q_held))
        loads.append(
            [pltpu.make_async_copy(x.at[:, span], y.at[:, span], sems.at[k, i]) for k, (x, y) in enumerate(pairs)]
        )
        for load in loads[-1]:
            load.start()
    left = jnp.zeros((2 * rank, rows), F32)
    stores = []
    for i, span in enumerate(spans):
        for load in loads[i]:
            load.wait()
        g, e = g_held[:, span], e_held[:, span]
        turned = (g.astype(F32) + e.astype(F32)).T
        out[2 * i, :cut, :] = turned[:cut]
        out[2 * i + 1, :cut, :] = turned[cut:]
        block = (pl.ds(2 * i, 2), pl.ds(0, cut))
        stores.append(pltpu.make_async_copy(out.at[block], result.at[block], out_sems.at[i]))
        stores[-1].start()
        high, low = split2(q_held[:, span])
        both = jnp.concatenate([high, low], axis=0)
        left = left + (dot(both, g, NT) + dot(both, e, NT))
    left = left[:rank] + left[rank:]
    for i in range(reps):
        out[i, cut : cut + extra, :] = left[extra * i : extra * (i + 1)]
        out[i, cut + extra :, :] = jnp.zeros((tall - cut - extra, rows), F32)
    block = (pl.ds(0, reps), pl.ds(cut, tall - cut))
    stores.append(pltpu.make_async_copy(out.at[block], result.at[block], out_sems.at[reps // 2]))
    stores[-1].start()
    for store in stores:
        store.wait()


def start(grads, errors, q_start, reps):
    rows, width = grads.shape
    tall = width // reps + 8
    return pl.pallas_call(
        start_kernel,
        in_specs=[HBM_SPEC] * 3,
        out_specs=HBM_SPEC,
        out_shape=jax.ShapeDtypeStruct((reps, tall, rows), F32),
        scratch_shapes=[
            pltpu.VMEM(grads.shape, BF16),
            pltpu.VMEM(errors.shape, BF16),
            pltpu.VMEM(q_start.shape, F32),
            pltpu.VMEM((reps, tall, rows), F32),
            pltpu.SemaphoreType.DMA((3, reps // 2)),
            pltpu.SemaphoreType.DMA((reps // 2 + 1,)),
        ],
        compiler_params=params(3 * VMEM),
        name="start",
    )(grads, errors, q_start)


def inverse_factor(gram_twice):
    rank, wide = gram_twice.shape
    step = 8
    count = rank // step
    row = lax.broadcasted_iota(jnp.int32, (step, wide), 0)
    col = lax.broadcasted_iota(jnp.int32, (step, wide), 1)

    def spread(x, k):
        return jnp.broadcast_to(x[:, k : k + 1], (step, wide))

    def line_of(x, j):
        return jnp.broadcast_to(x[j : j + 1, :], (step, wide))

    parts = [gram_twice[b * step : (b + 1) * step] for b in range(count)]
    near = [jnp.where(col == row + b * step, parts[b], 0.0) for b in range(count)]
    both = sum(jnp.where(col == row + (rank + b * step), parts[b], near[b]) for b in range(count))
    across = lax.rsqrt(jnp.sum(both, axis=0, keepdims=True))
    a = []
    for b in range(count):
        down = lax.rsqrt(jnp.sum(near[b], axis=1, keepdims=True))
        unit = (col == row + (rank + b * step)).astype(F32)
        a.append(jnp.where(col < rank, parts[b] * down * across, unit))

    done = []
    for p in range(count):
        panel = a[p]
        f = [spread(panel, p * step + j) for j in range(step)]
        pivots = jnp.ones((step, wide), F32)
        pairs = []
        for j in range(0, step, 2):
            x, z, y = line_of(f[j], j), line_of(f[j], j + 1), line_of(f[j + 1], j + 1)
            det = x * y - z * z
            inverse = 1.0 / det

            def solve(v):
                top, low = line_of(v, j), line_of(v, j + 1)
                return (y * top - z * low) * inverse, (x * low - z * top) * inverse

            below = [jnp.where(row > j + 1, f[j + i], 0.0) for i in range(2)]
            ahead = {}
            for t in range(j + 2, step):
                ahead[t] = solve(f[t])
                f[t] = f[t] - (below[0] * ahead[t][0] + below[1] * ahead[t][1])
            line = solve(panel)
            ratio = 1.0 / x
            second = line_of(panel, j + 1) - (z * ratio) * line_of(panel, j)
            panel = panel - (below[0] * line[0] + below[1] * line[1])
            panel = jnp.where(row == j + 1, second, panel)
            pivots = jnp.where(row == j, x, jnp.where(row == j + 1, det * ratio, pivots))
            pairs.append((line, ahead))
        done.append(jnp.where(col < rank, 0.0, panel * lax.rsqrt(pivots) * across))
        for b in range(p + 1, count):
            g = [spread(a[b], p * step + j) for j in range(step)]
            for j, (line, ahead) in zip(range(0, step, 2), pairs):
                for t in range(j + 2, step):
                    g[t] = g[t] - (g[j] * ahead[t][0] + g[j + 1] * ahead[t][1])
                a[b] = a[b] - (g[j] * line[0] + g[j + 1] * line[1])
    w = jnp.concatenate(done, axis=0)
    return w + pltpu.roll(w, rank, 1)


def gram_of(held, chunk):
    rank = held.shape[0] // 4
    total = jnp.zeros((3 * rank, 4 * rank), F32)
    for at in range(0, held.shape[1], chunk):
        x = held[:, at : at + chunk]
        total = total + dot(x[: 3 * rank], x, NT)
    total = total[:rank] + (total[rank : 2 * rank] + total[2 * rank :])
    near, far = total[:, : 2 * rank], total[:, 2 * rank :]
    return near + pltpu.roll(near, rank, 1) + far


def put(held, at, x):
    rank, n = x.shape
    high, mid, low = split3(x)
    span = pl.ds(at, n)
    held[:rank, span] = high
    held[rank : 2 * rank, span] = mid
    held[2 * rank : 3 * rank, span] = low
    held[3 * rank :, span] = low


def weights(w):
    rank = w.shape[0]
    col = lax.broadcasted_iota(jnp.int32, w.shape, 1)
    once = jnp.where(col < rank, w, 0.0)
    wide = jnp.concatenate([w, once], axis=1)
    return jnp.concatenate(split3(wide), axis=0)


CHUNK = 512


def right_of(held, high, low):
    rank = held.shape[0] // 4
    cut, n = high.shape
    one = jnp.zeros((2 * rank, cut), F32)
    two = jnp.zeros((rank, cut), F32)
    for at in range(0, n, CHUNK):
        x = held[: 2 * rank, at : at + CHUNK]
        one = one + dot(x, high[:, at : at + CHUNK], NT)
        two = two + dot(x[:rank], low[:, at : at + CHUNK], NT)
    return one[:rank] + (one[rank:] + two)


def planes(info, length, mine):
    upward = info[1] == (0 if mine else 1)
    columns = 2 * LANES

    def at(j):
        plane = lax.rem(info[0] + jnp.where(upward, length - j, 1 + j), length)
        return pl.multiple_of(plane * columns, columns)

    return at


def orthonormal(info, own, other, held):
    length = own.shape[0]
    for mine, blocks in ((True, own), (False, other)):
        at = planes(info, length, mine)
        for j in range(length // 2):
            put(held, at(j), jnp.concatenate([blocks[2 * j], blocks[2 * j + 1]], axis=1))
    left = weights(inverse_factor(gram_of(held, CHUNK)))
    for at in range(0, held.shape[1], CHUNK):
        y = dot(left, held[:, at : at + CHUNK], NN)
        put(held, at, y[: y.shape[0] // 3] + (y[y.shape[0] // 3 : 2 * y.shape[0] // 3] + y[2 * y.shape[0] // 3 :]))
    return inverse_factor(gram_of(held, CHUNK))


def right_factor(scale, second, held, high, low):
    left = second[:, : second.shape[0]] * scale
    right = right_of(held, high, low)
    return jnp.dot(left, right, precision=lax.Precision.HIGHEST, preferred_element_type=F32)


def next_left(info, q, high, low, out):
    length, rank, rows = out.shape
    q_high, q_low = split2(q)
    both = jnp.concatenate([q_high, q_low], axis=0)
    at = planes(info, length, True)
    for j in range(length // 2):
        span = pl.ds(at(j), 2 * rows)
        one = dot(both, high[:, span], NN)
        x = one[:rank] + (one[rank:] + dot(q_high, low[:, span], NN))
        out[2 * j] = x[:, :rows]
        out[2 * j + 1] = x[:, rows:]


def first_kernel(scale, info, own, other, total, total_other, out, high, low, held):
    half = total.shape[0]
    for mine, blocks in ((True, total), (False, total_other)):
        at = planes(info, 2 * half, mine)
        core = info[1] if mine else 1 - info[1]
        for j in range(half):
            for stream in range(2):
                side = core if stream == 0 else 1 - core
                span = pl.ds(pl.multiple_of(at(j) + side * LANES, LANES), LANES)
                high[:, span], low[:, span] = split2(blocks[j, stream])
    second = orthonormal(info, own, other, held)
    next_left(info, right_factor(scale, second, held, high, low), high, low, out)


def step_kernel(scale, info, own, other, high, low, out, held):
    second = orthonormal(info, own, other, held)
    next_left(info, right_factor(scale, second, held, high, low), high, low, out)


def last_kernel(scale, info, own, other, high, low, out, basis, held):
    length, rank, rows = own.shape
    second = orthonormal(info, own, other, held)
    q = right_factor(scale, second, held, high, low)
    half = rank // 2
    quarter = half // 2
    rest = jnp.concatenate([q[:, 2 * LANES :], jnp.zeros_like(q[:, 2 * LANES :])], axis=1)
    for core in range(2):
        span = slice(core * half, (core + 1) * half)
        out[core, :half] = q[span, :LANES]
        out[core, half : 2 * half] = q[span, LANES : 2 * LANES]
        tail = rest[span]
        out[core, 2 * half :] = tail[:quarter] + pltpu.roll(tail[quarter:], LANES // 2, 1)
    at = pl.multiple_of((2 * info[0] + info[1]) * rows, rows)
    y = dot(weights(second), held[:, pl.ds(at, rows)], NN)
    basis[...] = y[:rank] + (y[rank : 2 * rank] + y[2 * rank :])


def held_scratch(own):
    length, rank, rows = own.shape
    return [pltpu.VMEM((4 * rank, 2 * length * rows), BF16)]


def first(scale, info, own, other, total, total_other):
    length, rank, rows = own.shape
    whole = jax.ShapeDtypeStruct((total.shape[2], 2 * length * rows), BF16)
    return pl.pallas_call(
        functools.partial(first_kernel, scale),
        in_specs=[SMEM_SPEC] + [VMEM_SPEC] * 4,
        out_shape=[jax.ShapeDtypeStruct(own.shape, F32), whole, whole],
        scratch_shapes=held_scratch(own),
        compiler_params=params(),
        name="first",
    )(info, own, other, total, total_other)


def step(scale, info, own, other, high, low):
    return pl.pallas_call(
        functools.partial(step_kernel, scale),
        in_specs=[SMEM_SPEC] + [VMEM_SPEC] * 4,
        out_shape=jax.ShapeDtypeStruct(own.shape, F32),
        scratch_shapes=held_scratch(own),
        compiler_params=params(),
        name="step",
    )(info, own, other, high, low)


def last(scale, info, own, other, high, low):
    length, rank, rows = own.shape
    shapes = [(2, 5 * rank // 4, LANES), (rank, rows)]
    return pl.pallas_call(
        functools.partial(last_kernel, scale),
        in_specs=[SMEM_SPEC] + [VMEM_SPEC] * 4,
        out_shape=[jax.ShapeDtypeStruct(x, F32) for x in shapes],
        scratch_shapes=held_scratch(own),
        compiler_params=params(),
        name="last",
    )(info, own, other, high, low)


def columns_of(top, low):
    half = top.shape[0] * 2 // 5
    quarter = half // 2
    lane = lax.broadcasted_iota(jnp.int32, (quarter, LANES), 1)
    blocks = []
    for x in (top, low):
        tail = x[2 * half :]
        upper = jnp.where(lane < LANES // 2, tail, 0.0)
        lower = jnp.where(lane < LANES // 2, pltpu.roll(tail, LANES // 2, 1), 0.0)
        blocks.append((x[:half], x[half : 2 * half], jnp.concatenate([upper, lower], axis=0)))
    return [jnp.concatenate([a, b], axis=0) for a, b in zip(*blocks)]


def finish_kernel(flag, grads, errors, own, other, basis, new_errors, factor_q):
    first_core = flag[0] == 0
    turned = basis[...].T
    b_high, b_low = split2(turned)
    left = jnp.concatenate([b_high, b_high, b_low], axis=1)
    wide = 5 * LANES
    lane = lax.broadcasted_iota(jnp.int32, (basis.shape[0], LANES), 1)
    for i in range(own.shape[0] // 2):
        even, odd = [
            columns_of(jnp.where(first_core, own[j], other[j]), jnp.where(first_core, other[j], own[j]))
            for j in (2 * i, 2 * i + 1)
        ]
        turn = [pltpu.roll(x, LANES // 2, 1) for x in odd]
        low_lane = lane < LANES // 2
        q = jnp.concatenate(
            [
                even[0],
                even[1],
                jnp.where(low_lane, even[2], turn[0]),
                jnp.where(low_lane, turn[0], turn[1]),
                jnp.where(low_lane, turn[1], turn[2]),
            ],
            axis=1,
        )
        span = slice(i * wide, (i + 1) * wide)
        factor_q[:, span] = q
        q_high, q_low = split2(q)
        product = dot(left, jnp.concatenate([q_high, q_low, q_high], axis=0), NN)
        merged = grads[:, span].astype(F32) + errors[:, span].astype(F32)
        new_errors[:, span] = (merged - product).astype(BF16)


def finish(flag, grads, errors, own, other, basis):
    rows, width = grads.shape
    reps, tall, lanes = own.shape
    rank = basis.shape[0]
    steps = 4
    cols = pl.BlockSpec((rows, width // steps), lambda i: (0, i))
    piece = pl.BlockSpec((reps // steps, tall, lanes), lambda i: (i, 0, 0))
    return pl.pallas_call(
        finish_kernel,
        grid=(steps,),
        in_specs=[SMEM_SPEC, cols, cols, piece, piece, pl.BlockSpec((rank, rows), lambda i: (0, 0))],
        out_specs=[cols, pl.BlockSpec((rank, width // steps), lambda i: (0, i))],
        out_shape=[jax.ShapeDtypeStruct((rows, width), BF16), jax.ShapeDtypeStruct((rank, width), F32)],
        compiler_params=params(),
        name="finish",
    )(flag, grads, errors, own, other, basis)


def exchange(chunks, axis):
    return lax.all_to_all(chunks, axis, 0, 0)


def gather(block, axis, count):
    return exchange(jnp.broadcast_to(block[None], (count,) + block.shape), axis)


def swap_cores(block):
    return lax.ppermute(block, "core", [(0, 1), (1, 0)])


def ring(block, length):
    half = length // 2
    up = [(2 * i, 2 * ((i + 1) % length)) for i in range(length)]
    down = [(2 * i + 1, 2 * ((i - 1) % length) + 1) for i in range(length)]
    blocks = [block]
    for s in range(half):
        blocks.append(lax.ppermute(blocks[-1], ("z", "core"), up + down if s < half - 1 else down))
    return blocks


def body(grads, errors, q_start):
    grads, errors = grads[0], errors[0]
    rows, width = grads.shape
    rank = q_start.shape[0]
    reps, length = lax.axis_size("rep"), lax.axis_size("z")
    core, place = lax.axis_index("core"), lax.axis_index("z")
    cut, extra = width // reps, rank // reps
    scale = 1.0 / reps
    flag = core.reshape(1).astype(jnp.int32)
    info = jnp.stack([place, core]).astype(jnp.int32)

    block = jnp.sum(exchange(start(grads, errors, q_start, reps), "rep"), axis=0)
    streams = ring(block, length), ring(swap_cores(block), length)
    held = jnp.stack(
        [jnp.stack([jnp.where(core == 0, x[j], x[j + 1]) for x in streams]) for j in range(length // 2)]
    )
    total = held[:, :, :cut]
    piece = held[:, :, cut : cut + extra]
    piece = jnp.where(core == 0, piece, piece[:, ::-1]).reshape(length * extra, rows)
    own = gather(piece, "rep", reps).reshape(reps, length, extra, rows)
    own = own.transpose(1, 0, 2, 3).reshape(length, rank, rows)
    partial, high, low = first(scale, info, own, swap_cores(own), total, swap_cores(total))
    for turn in range(ITERS - 1):
        own = gather(jnp.sum(exchange(partial, "rep"), axis=0), "rep", reps)
        if turn < ITERS - 2:
            partial = step(scale, info, own, swap_cores(own), high, low)
    part_q, basis = last(scale, info, own, swap_cores(own), high, low)
    own_q = gather(lax.dynamic_index_in_dim(part_q, core, 0, False), "rep", reps)
    new_errors, factor_q = finish(flag, grads, errors, own_q, swap_cores(own_q), basis)
    return new_errors[None], factor_q


def solution(mesh):
    reps, count = mesh.devices.shape
    split = Mesh(mesh.devices.reshape(reps, count // 2, 2), ("rep", "z", "core"))
    placed = P("rep", ("z", "core"), None)
    return jax.shard_map(
        body, mesh=split, in_specs=(placed, placed, P()), out_specs=(placed, P()), check_vma=False
    )
```

```python
import functools

import jax
import jax.numpy as jnp
from jax import lax
from jax.experimental import pallas as pl
from jax.experimental.pallas import tpu as pltpu
from jax.sharding import Mesh, PartitionSpec as P

ITERS = 3
F32 = jnp.float32
BF16 = jnp.bfloat16
LANES = 128
VMEM = 20 * 1024 * 1024
SMEM_SPEC = pl.BlockSpec(memory_space=pltpu.SMEM)
VMEM_SPEC = pl.BlockSpec(memory_space=pltpu.VMEM)
HBM_SPEC = pl.BlockSpec(memory_space=pltpu.HBM)
NT = (((1,), (1,)), ((), ()))
NN = (((1,), (0,)), ((), ()))


def dot(a, b, dims):
    return lax.dot_general(a, b, dims, preferred_element_type=F32)


def split2(x):
    high = x.astype(BF16)
    return high, (x - high.astype(F32)).astype(BF16)


def split3(x):
    high = x.astype(BF16)
    rest = x - high.astype(F32)
    mid = rest.astype(BF16)
    return high, mid, (rest - mid.astype(F32)).astype(BF16)


def params(limit=VMEM):
    return pltpu.CompilerParams(vmem_limit_bytes=limit)


def start_kernel(grads, errors, q_start, result, g_held, e_held, q_held, out, sems, out_sems):
    reps, tall, rows = out.shape
    rank, width = q_start.shape
    cut = width // reps
    extra = rank // reps
    spans = [pl.ds(2 * cut * i, 2 * cut) for i in range(reps // 2)]
    loads = []
    for i, span in enumerate(spans):
        pairs = ((grads, g_held), (errors, e_held), (q_start, q_held))
        loads.append(
            [pltpu.make_async_copy(x.at[:, span], y.at[:, span], sems.at[k, i]) for k, (x, y) in enumerate(pairs)]
        )
        for load in loads[-1]:
            load.start()
    left = jnp.zeros((2 * rank, rows), F32)
    stores = []
    for i, span in enumerate(spans):
        for load in loads[i]:
            load.wait()
        g, e = g_held[:, span], e_held[:, span]
        turned = (g.astype(F32) + e.astype(F32)).T
        out[2 * i, :cut, :] = turned[:cut]
        out[2 * i + 1, :cut, :] = turned[cut:]
        block = (pl.ds(2 * i, 2), pl.ds(0, cut))
        stores.append(pltpu.make_async_copy(out.at[block], result.at[block], out_sems.at[i]))
        stores[-1].start()
        high, low = split2(q_held[:, span])
        both = jnp.concatenate([high, low], axis=0)
        left = left + (dot(both, g, NT) + dot(both, e, NT))
    left = left[:rank] + left[rank:]
    for i in range(reps):
        out[i, cut : cut + extra, :] = left[extra * i : extra * (i + 1)]
        out[i, cut + extra :, :] = jnp.zeros((tall - cut - extra, rows), F32)
    block = (pl.ds(0, reps), pl.ds(cut, tall - cut))
    stores.append(pltpu.make_async_copy(out.at[block], result.at[block], out_sems.at[reps // 2]))
    stores[-1].start()
    for store in stores:
        store.wait()


def start(grads, errors, q_start, reps):
    rows, width = grads.shape
    tall = width // reps + 8
    return pl.pallas_call(
        start_kernel,
        in_specs=[HBM_SPEC] * 3,
        out_specs=HBM_SPEC,
        out_shape=jax.ShapeDtypeStruct((reps, tall, rows), F32),
        scratch_shapes=[
            pltpu.VMEM(grads.shape, BF16),
            pltpu.VMEM(errors.shape, BF16),
            pltpu.VMEM(q_start.shape, F32),
            pltpu.VMEM((reps, tall, rows), F32),
            pltpu.SemaphoreType.DMA((3, reps // 2)),
            pltpu.SemaphoreType.DMA((reps // 2 + 1,)),
        ],
        compiler_params=params(3 * VMEM),
        name="start",
    )(grads, errors, q_start)


def inverse_factor(gram_twice, beside=None):
    rank, wide = gram_twice.shape
    step = 8
    count = rank // step
    row = lax.broadcasted_iota(jnp.int32, (step, wide), 0)
    col = lax.broadcasted_iota(jnp.int32, (step, wide), 1)

    def spread(x, k):
        return jnp.broadcast_to(x[:, k : k + 1], (step, wide))

    def line_of(x, j):
        return jnp.broadcast_to(x[j : j + 1, :], (step, wide))

    parts = [gram_twice[b * step : (b + 1) * step] for b in range(count)]
    near = [jnp.where(col == row + b * step, parts[b], 0.0) for b in range(count)]
    both = sum(jnp.where(col == row + (rank + b * step), parts[b], near[b]) for b in range(count))
    across = lax.rsqrt(jnp.sum(both, axis=0, keepdims=True))
    a = []
    for b in range(count):
        down = lax.rsqrt(jnp.sum(near[b], axis=1, keepdims=True))
        unit = (col == row + (rank + b * step)).astype(F32)
        a.append(jnp.where(col < rank, parts[b] * down * across, unit))

    done = []
    for p in range(count):
        if beside is not None:
            beside(p, count)
        panel = a[p]
        f = [spread(panel, p * step + j) for j in range(step)]
        pivots = jnp.ones((step, wide), F32)
        pairs = []
        for j in range(0, step, 2):
            x, z, y = line_of(f[j], j), line_of(f[j], j + 1), line_of(f[j + 1], j + 1)
            det = x * y - z * z
            inverse = 1.0 / det

            def solve(v):
                top, low = line_of(v, j), line_of(v, j + 1)
                return (y * top - z * low) * inverse, (x * low - z * top) * inverse

            below = [jnp.where(row > j + 1, f[j + i], 0.0) for i in range(2)]
            ahead = {}
            for t in range(j + 2, step):
                ahead[t] = solve(f[t])
                f[t] = f[t] - (below[0] * ahead[t][0] + below[1] * ahead[t][1])
            line = solve(panel)
            ratio = 1.0 / x
            second = line_of(panel, j + 1) - (z * ratio) * line_of(panel, j)
            panel = panel - (below[0] * line[0] + below[1] * line[1])
            panel = jnp.where(row == j + 1, second, panel)
            pivots = jnp.where(row == j, x, jnp.where(row == j + 1, det * ratio, pivots))
            pairs.append((line, ahead))
        done.append(jnp.where(col < rank, 0.0, panel * lax.rsqrt(pivots) * across))
        for b in range(p + 1, count):
            g = [spread(a[b], p * step + j) for j in range(step)]
            for j, (line, ahead) in zip(range(0, step, 2), pairs):
                for t in range(j + 2, step):
                    g[t] = g[t] - (g[j] * ahead[t][0] + g[j + 1] * ahead[t][1])
                a[b] = a[b] - (g[j] * line[0] + g[j + 1] * line[1])
    w = jnp.concatenate(done, axis=0)
    return w + pltpu.roll(w, rank, 1)


def gram_of(held, chunk):
    rank = held.shape[0] // 4
    total = jnp.zeros((3 * rank, 4 * rank), F32)
    for at in range(0, held.shape[1], chunk):
        x = held[:, at : at + chunk]
        total = total + dot(x[: 3 * rank], x, NT)
    total = total[:rank] + (total[rank : 2 * rank] + total[2 * rank :])
    near, far = total[:, : 2 * rank], total[:, 2 * rank :]
    return near + pltpu.roll(near, rank, 1) + far


def put(held, at, x):
    rank, n = x.shape
    high, mid, low = split3(x)
    span = pl.ds(at, n)
    held[:rank, span] = high
    held[rank : 2 * rank, span] = mid
    held[2 * rank : 3 * rank, span] = low
    held[3 * rank :, span] = low


def weights(w):
    rank = w.shape[0]
    col = lax.broadcasted_iota(jnp.int32, w.shape, 1)
    once = jnp.where(col < rank, w, 0.0)
    wide = jnp.concatenate([w, once], axis=1)
    return jnp.concatenate(split3(wide), axis=0)


CHUNK = 512


class Right:
    def __init__(self, held, high, low):
        rank = held.shape[0] // 4
        self.refs = held, high, low
        self.one = jnp.zeros((2 * rank, high.shape[0]), F32)
        self.two = jnp.zeros((rank, high.shape[0]), F32)

    def add(self, p, count):
        held, high, low = self.refs
        size = high.shape[1] // count
        x = held[: 2 * self.two.shape[0], p * size : (p + 1) * size]
        span = slice(p * size, (p + 1) * size)
        self.one = self.one + dot(x, high[:, span], NT)
        self.two = self.two + dot(x[: self.two.shape[0]], low[:, span], NT)

    def total(self):
        rank = self.two.shape[0]
        return self.one[:rank] + (self.one[rank:] + self.two)


def planes(info, length, mine):
    upward = info[1] == (0 if mine else 1)
    columns = 2 * LANES

    def at(j):
        plane = lax.rem(info[0] + jnp.where(upward, length - j, 1 + j), length)
        return pl.multiple_of(plane * columns, columns)

    return at


def orthonormal(info, own, other, held, high, low, beside=None):
    length, rank = own.shape[:2]
    for mine, blocks in ((True, own), (False, other)):
        at = planes(info, length, mine)
        for j in range(length // 2):
            put(held, at(j), jnp.concatenate([blocks[2 * j], blocks[2 * j + 1]], axis=1))
    left = weights(inverse_factor(gram_of(held, CHUNK), beside))
    for at in range(0, held.shape[1], CHUNK):
        y = dot(left, held[:, at : at + CHUNK], NN)
        put(held, at, y[:rank] + (y[rank : 2 * rank] + y[2 * rank :]))
    right = Right(held, high, low)
    second = inverse_factor(gram_of(held, CHUNK), right.add)
    return second, right.total()


def right_factor(scale, second, right):
    left = second[:, : second.shape[0]] * scale
    return jnp.dot(left, right, precision=lax.Precision.HIGHEST, preferred_element_type=F32)


def next_left(info, q, high, low, out):
    length, rank, rows = out.shape
    q_high, q_low = split2(q)
    both = jnp.concatenate([q_high, q_low], axis=0)
    at = planes(info, length, True)
    for j in range(length // 2):
        span = pl.ds(at(j), 2 * rows)
        one = dot(both, high[:, span], NN)
        x = one[:rank] + (one[rank:] + dot(q_high, low[:, span], NN))
        out[2 * j] = x[:, :rows]
        out[2 * j + 1] = x[:, rows:]


def first_kernel(scale, info, own, other, total, total_other, out, high, low, held):
    half = total.shape[0]

    def split(p, count):
        for mine, blocks in ((True, total), (False, total_other)):
            at = planes(info, 2 * half, mine)
            core = info[1] if mine else 1 - info[1]
            for j in range(p * half // count, (p + 1) * half // count):
                for stream in range(2):
                    side = core if stream == 0 else 1 - core
                    span = pl.ds(pl.multiple_of(at(j) + side * LANES, LANES), LANES)
                    high[:, span], low[:, span] = split2(blocks[j, stream])

    second, right = orthonormal(info, own, other, held, high, low, split)
    next_left(info, right_factor(scale, second, right), high, low, out)


def step_kernel(scale, info, own, other, high, low, out, held):
    second, right = orthonormal(info, own, other, held, high, low)
    next_left(info, right_factor(scale, second, right), high, low, out)


def last_kernel(scale, info, own, other, high, low, out, basis, held):
    length, rank, rows = own.shape
    second, right = orthonormal(info, own, other, held, high, low)
    q = right_factor(scale, second, right)
    half = rank // 2
    quarter = half // 2
    rest = jnp.concatenate([q[:, 2 * LANES :], jnp.zeros_like(q[:, 2 * LANES :])], axis=1)
    for core in range(2):
        span = slice(core * half, (core + 1) * half)
        out[core, :half] = q[span, :LANES]
        out[core, half : 2 * half] = q[span, LANES : 2 * LANES]
        tail = rest[span]
        out[core, 2 * half :] = tail[:quarter] + pltpu.roll(tail[quarter:], LANES // 2, 1)
    at = pl.multiple_of((2 * info[0] + info[1]) * rows, rows)
    y = dot(weights(second), held[:, pl.ds(at, rows)], NN)
    basis[...] = y[:rank] + (y[rank : 2 * rank] + y[2 * rank :])


def held_scratch(own):
    length, rank, rows = own.shape
    return [pltpu.VMEM((4 * rank, 2 * length * rows), BF16)]


def first(scale, info, own, other, total, total_other):
    length, rank, rows = own.shape
    whole = jax.ShapeDtypeStruct((total.shape[2], 2 * length * rows), BF16)
    return pl.pallas_call(
        functools.partial(first_kernel, scale),
        in_specs=[SMEM_SPEC] + [VMEM_SPEC] * 4,
        out_shape=[jax.ShapeDtypeStruct(own.shape, F32), whole, whole],
        scratch_shapes=held_scratch(own),
        compiler_params=params(),
        name="first",
    )(info, own, other, total, total_other)


def step(scale, info, own, other, high, low):
    return pl.pallas_call(
        functools.partial(step_kernel, scale),
        in_specs=[SMEM_SPEC] + [VMEM_SPEC] * 4,
        out_shape=jax.ShapeDtypeStruct(own.shape, F32),
        scratch_shapes=held_scratch(own),
        compiler_params=params(),
        name="step",
    )(info, own, other, high, low)


def last(scale, info, own, other, high, low):
    length, rank, rows = own.shape
    shapes = [(2, 5 * rank // 4, LANES), (rank, rows)]
    return pl.pallas_call(
        functools.partial(last_kernel, scale),
        in_specs=[SMEM_SPEC] + [VMEM_SPEC] * 4,
        out_shape=[jax.ShapeDtypeStruct(x, F32) for x in shapes],
        scratch_shapes=held_scratch(own),
        compiler_params=params(),
        name="last",
    )(info, own, other, high, low)


def columns_of(top, low):
    half = top.shape[0] * 2 // 5
    quarter = half // 2
    lane = lax.broadcasted_iota(jnp.int32, (quarter, LANES), 1)
    blocks = []
    for x in (top, low):
        tail = x[2 * half :]
        upper = jnp.where(lane < LANES // 2, tail, 0.0)
        lower = jnp.where(lane < LANES // 2, pltpu.roll(tail, LANES // 2, 1), 0.0)
        blocks.append((x[:half], x[half : 2 * half], jnp.concatenate([upper, lower], axis=0)))
    return [jnp.concatenate([a, b], axis=0) for a, b in zip(*blocks)]


def finish_kernel(flag, grads, errors, own, other, basis, new_errors, factor_q):
    first_core = flag[0] == 0
    turned = basis[...].T
    b_high, b_low = split2(turned)
    left = jnp.concatenate([b_high, b_high, b_low], axis=1)
    wide = 5 * LANES
    lane = lax.broadcasted_iota(jnp.int32, (basis.shape[0], LANES), 1)
    for i in range(own.shape[0] // 2):
        even, odd = [
            columns_of(jnp.where(first_core, own[j], other[j]), jnp.where(first_core, other[j], own[j]))
            for j in (2 * i, 2 * i + 1)
        ]
        turn = [pltpu.roll(x, LANES // 2, 1) for x in odd]
        low_lane = lane < LANES // 2
        q = jnp.concatenate(
            [
                even[0],
                even[1],
                jnp.where(low_lane, even[2], turn[0]),
                jnp.where(low_lane, turn[0], turn[1]),
                jnp.where(low_lane, turn[1], turn[2]),
            ],
            axis=1,
        )
        span = slice(i * wide, (i + 1) * wide)
        factor_q[:, span] = q
        q_high, q_low = split2(q)
        product = dot(left, jnp.concatenate([q_high, q_low, q_high], axis=0), NN)
        merged = grads[:, span].astype(F32) + errors[:, span].astype(F32)
        new_errors[:, span] = (merged - product).astype(BF16)


def finish(flag, grads, errors, own, other, basis):
    rows, width = grads.shape
    reps, tall, lanes = own.shape
    rank = basis.shape[0]
    steps = 4
    cols = pl.BlockSpec((rows, width // steps), lambda i: (0, i))
    piece = pl.BlockSpec((reps // steps, tall, lanes), lambda i: (i, 0, 0))
    return pl.pallas_call(
        finish_kernel,
        grid=(steps,),
        in_specs=[SMEM_SPEC, cols, cols, piece, piece, pl.BlockSpec((rank, rows), lambda i: (0, 0))],
        out_specs=[cols, pl.BlockSpec((rank, width // steps), lambda i: (0, i))],
        out_shape=[jax.ShapeDtypeStruct((rows, width), BF16), jax.ShapeDtypeStruct((rank, width), F32)],
        compiler_params=params(),
        name="finish",
    )(flag, grads, errors, own, other, basis)


def exchange(chunks, axis):
    return lax.all_to_all(chunks, axis, 0, 0)


def gather(block, axis, count):
    return exchange(jnp.broadcast_to(block[None], (count,) + block.shape), axis)


def swap_cores(block):
    return lax.ppermute(block, "core", [(0, 1), (1, 0)])


def ring(block, length):
    half = length // 2
    up = [(2 * i, 2 * ((i + 1) % length)) for i in range(length)]
    down = [(2 * i + 1, 2 * ((i - 1) % length) + 1) for i in range(length)]
    blocks = [block]
    for s in range(half):
        blocks.append(lax.ppermute(blocks[-1], ("z", "core"), up + down if s < half - 1 else down))
    return blocks


def body(grads, errors, q_start):
    grads, errors = grads[0], errors[0]
    rows, width = grads.shape
    rank = q_start.shape[0]
    reps, length = lax.axis_size("rep"), lax.axis_size("z")
    core, place = lax.axis_index("core"), lax.axis_index("z")
    cut, extra = width // reps, rank // reps
    scale = 1.0 / reps
    flag = core.reshape(1).astype(jnp.int32)
    info = jnp.stack([place, core]).astype(jnp.int32)

    block = jnp.sum(exchange(start(grads, errors, q_start, reps), "rep"), axis=0)
    streams = ring(block, length), ring(swap_cores(block), length)
    held = jnp.stack(
        [jnp.stack([jnp.where(core == 0, x[j], x[j + 1]) for x in streams]) for j in range(length // 2)]
    )
    total = held[:, :, :cut]
    piece = held[:, :, cut : cut + extra]
    piece = jnp.where(core == 0, piece, piece[:, ::-1]).reshape(length * extra, rows)
    own = gather(piece, "rep", reps).reshape(reps, length, extra, rows)
    own = own.transpose(1, 0, 2, 3).reshape(length, rank, rows)
    partial, high, low = first(scale, info, own, swap_cores(own), total, swap_cores(total))
    for turn in range(ITERS - 1):
        own = gather(jnp.sum(exchange(partial, "rep"), axis=0), "rep", reps)
        if turn < ITERS - 2:
            partial = step(scale, info, own, swap_cores(own), high, low)
    part_q, basis = last(scale, info, own, swap_cores(own), high, low)
    own_q = gather(lax.dynamic_index_in_dim(part_q, core, 0, False), "rep", reps)
    new_errors, factor_q = finish(flag, grads, errors, own_q, swap_cores(own_q), basis)
    return new_errors[None], factor_q


def solution(mesh):
    reps, count = mesh.devices.shape
    split = Mesh(mesh.devices.reshape(reps, count // 2, 2), ("rep", "z", "core"))
    placed = P("rep", ("z", "core"), None)
    return jax.shard_map(
        body, mesh=split, in_specs=(placed, placed, P()), out_specs=(placed, P()), check_vma=False
    )
```
